512 devices in a mesh: dp: 64 (over z, y), mp: 8 (over x, core).
Axes of the slice: x: 4, y: 8, z: 8, core: 2. Of those that a mesh axis runs over, the one named last changes fastest.
Arguments:
- hidden_in: bfloat16 [8192, 4096], P('dp', 'mp'), may hold values from -100 to 100
- queries: bfloat16 [8192, 4096], P('dp', 'mp'), may hold values from -100 to 100
- image_kv: bfloat16 [128, 2, 32, 4096], P('dp', None, None, 'mp'), may hold values from -6 to 6
- image_owner: int32 [128], replicated, may hold values from 0 to 127, as said below
- citations: int32 [64, 32], replicated, may hold values from 0 to 127, as said below
- cite_mask: int32 [8192, 32], P('dp'), may hold values from 0 to 1, as said below
- gate_scalars: float32 [1], replicated, may hold values from 0.3 to 1.2
- norm_gain: float32 [4096], replicated, may hold values from 0.5 to 1.5
- upstream: bfloat16 [8192, 4096], P('dp', 'mp'), may hold values from -100 to 100
Outputs:
- block_out: bfloat16 [8192, 4096], P('dp', 'mp')
- normed_out: bfloat16 [8192, 4096], P('dp', 'mp')
- hidden_grad: bfloat16 [8192, 4096], P('dp', 'mp')
- query_grad: bfloat16 [8192, 4096], P('dp', 'mp')
- image_kv_grad: bfloat16 [128, 2, 32, 4096], P('dp', None, None, 'mp')
The draws below stay inside these ranges and needn't reach their ends.
Inputs may be any that keep to these rules, and one draw needn't show every extreme that they name: `image_owner`: a permutation of the 128 rows of image_kv. `citations`: each row names 32 different image ids, and no two of them are stored by the same encoder shard (image_owner[id] // 2 differ). `cite_mask`: every text token has at least one 1.
All inputs are finite; a program needn't handle non-finite values.
Results may differ from the reference program's by a relative error of at most 0.0095.
Values may be sent and summed in bfloat16 or wider, within the bound.
A program may use at most 64 MiB of HBM per device.

```python
import jax
import jax.numpy as jnp
from jax import lax

D = 4096
HEAD_DIM = 128
IT = 32
IMG_DEV = 2
TOK_DEV = 128
HEADS = 32
TOKENS = 8192
NI = 128
CITE = 32
N_DP = 64


def shared_rows(key):
    first, second = jax.random.split(key, 2)
    columns = jnp.arange(D, dtype=jnp.float32)[None, :] / (D - 1)
    rough = jnp.exp(jax.random.uniform(second, (1, D), jnp.float32, -0.35, 0.35))
    column_scale = jnp.exp(jnp.log(3.0) * columns) * rough
    values = jnp.clip(jax.random.normal(first, (TOKENS, D), jnp.float32), -4.0, 4.0)
    return values * column_scale


def storage_order(key):
    return jax.random.permutation(jax.random.fold_in(key, 101), NI).astype(jnp.int32)


def draw_hidden_in(key, part):
    base = shared_rows(key)
    return jnp.clip(base, -96.0, 96.0).astype(jnp.bfloat16)


def draw_upstream(key, part):
    base = shared_rows(key)
    key = jax.random.fold_in(key, 13)
    first, second = jax.random.split(key)
    weights = jax.random.uniform(first, (TOKENS, 1), jnp.float32, 0.4, 1.2)
    noise = jnp.clip(jax.random.normal(second, (TOKENS, D), jnp.float32), -4.0, 4.0)
    return jnp.clip(weights * base + noise, -96.0, 96.0).astype(jnp.bfloat16)


def draw_queries(key, part):
    key = jax.random.fold_in(key, 3)
    first = jax.random.fold_in(key, 0)
    values = jnp.clip(jax.random.normal(first, (TOKENS, D), jnp.float32), -4.0, 4.0)
    return values.astype(jnp.bfloat16)


def draw_image_owner(key, part):
    return storage_order(key)


def draw_citations(key, part):
    stored_at = storage_order(key)
    key = jax.random.fold_in(key, 5)
    first, second = jax.random.split(key)
    keys = jax.random.split(first, N_DP)
    owners = jax.vmap(lambda one: jax.random.permutation(one, N_DP))(keys)[:, :CITE].astype(jnp.int32)
    slots = jax.random.randint(second, (N_DP, CITE), 0, IMG_DEV).astype(jnp.int32)
    stored = owners * IMG_DEV + slots
    inverse = jnp.zeros((NI,), jnp.int32).at[stored_at].set(jnp.arange(NI, dtype=jnp.int32))
    return inverse[stored].astype(jnp.int32)


def draw_cite_mask(key, part):
    key = jax.random.fold_in(key, 7)
    first, second, third = jax.random.split(key, 3)
    levels = jax.random.randint(first, (N_DP, 1, 1), 1, 4)
    levels = jnp.broadcast_to(levels, (N_DP, TOK_DEV, CITE)).reshape(TOKENS, CITE)
    coins = jax.random.randint(second, (TOKENS, CITE), 0, 4)
    forced = jax.random.randint(third, (TOKENS, 1), 0, CITE)
    places = jnp.arange(CITE, dtype=jnp.int32)[None, :]
    chosen = (coins < levels) | (places == forced)
    return chosen.astype(jnp.int32)


def block_scale(rng, dims, shards, low, top_value):
    def one(dim, blocks):
        steps = jax.random.uniform(jax.random.fold_in(jax.random.fold_in(rng, 6), dim), (blocks,), jnp.float32, low / len(shards), top_value / len(shards))
        return jnp.repeat(jnp.exp(steps), dims[dim] // blocks).reshape((-1,) + (1,) * (len(dims) - dim - 1))

    loudness = one(*shards[0])
    for cut in shards[1:]:
        loudness = loudness * one(*cut)
    return loudness


def gaussian(rng, dims, width, bound, cuts=(), held_as=jnp.bfloat16):
    result = width * jax.random.normal(rng, dims, jnp.float32)
    if cuts:
        result = result * block_scale(rng, dims, cuts, -0.22, 0.18)
    return jnp.clip(result, -bound, bound).astype(held_as)


def setup_inputs(seed: int = 0) -> dict:
    seeds = jax.random.split(jax.random.key(seed), 10)
    return {
        "hidden_in": draw_hidden_in(jax.random.fold_in(seeds[9], 71), 0),
        "queries": draw_queries(jax.random.fold_in(seeds[9], 71), 0),
        "image_kv": gaussian(seeds[2], (NI, 2, IT, D), 1.0, 6.0, ((0, 64), (3, 8))),
        "image_owner": draw_image_owner(jax.random.fold_in(seeds[9], 71), 0),
        "citations": draw_citations(jax.random.fold_in(seeds[9], 71), 0),
        "cite_mask": draw_cite_mask(jax.random.fold_in(seeds[9], 71), 0),
        "gate_scalars": jnp.clip(jax.random.uniform(seeds[6], (1,), jnp.float32, 0.3, 1.2), 0.3, 1.2),
        "norm_gain": jnp.clip(1.0 + 0.1 * jax.random.normal(seeds[7], (D,), jnp.float32), 0.5, 1.5),
        "upstream": draw_upstream(jax.random.fold_in(seeds[9], 71), 0),
    }


def rounded(value):
    return lax.optimization_barrier(value.astype(jnp.bfloat16)).astype(jnp.float32)

def shard_tensors(image_kv, image_owner, cite_row, mask_block):
    stored = image_owner[cite_row].astype(jnp.int32)
    selected = image_kv[stored]
    keys = selected[:, 0].reshape(CITE * IT, HEADS, HEAD_DIM).astype(jnp.float32)
    values = selected[:, 1].reshape(CITE * IT, HEADS, HEAD_DIM).astype(jnp.float32)
    allowed = jnp.broadcast_to(mask_block[:, :, None] > 0, (TOK_DEV, CITE, IT)).reshape(TOK_DEV, CITE * IT)
    return (stored, keys, values, allowed)

def attention_probs(query_rows, keys, allowed):
    scores = jnp.einsum('thd,khd->htk', query_rows, keys) * HEAD_DIM ** (-0.5)
    scores = jnp.where(allowed[None], scores, jnp.float32(-1e+30))
    return jax.nn.softmax(scores, axis=-1)

def reference(hidden_in, queries, image_kv, image_owner, citations, cite_mask, gate_scalars, norm_gain, upstream):
    query_blocks = queries.reshape(N_DP, TOK_DEV, HEADS, HEAD_DIM)
    mask_blocks = cite_mask.reshape(N_DP, TOK_DEV, CITE)
    gate_attn = jnp.tanh(gate_scalars[0])

    def forward_shard(item):
        query_rows, mask_block, cite_row = item
        stored, keys, values, allowed = shard_tensors(image_kv, image_owner, cite_row, mask_block)
        probs = attention_probs(query_rows.astype(jnp.float32), keys, allowed)
        return jnp.einsum('htk,khd->thd', rounded(probs), values).reshape(TOK_DEV, D)
    attended = lax.map(forward_shard, (query_blocks, mask_blocks, citations)).reshape(TOKENS, D)
    block_out = (hidden_in.astype(jnp.float32) + gate_attn * attended).astype(jnp.bfloat16)
    wide = block_out.astype(jnp.float32)
    inverse = lax.rsqrt(lax.optimization_barrier(jnp.sum(wide * wide, axis=-1, keepdims=True)) / D + 1e-05)
    normed_out = (wide * inverse * norm_gain).astype(jnp.bfloat16)
    weighted = norm_gain * upstream.astype(jnp.float32)
    inner = lax.optimization_barrier(jnp.sum(weighted * wide, axis=-1, keepdims=True))
    hidden_total = inverse * weighted - wide * inverse ** 3 * inner / D
    hidden_grad = hidden_total.astype(jnp.bfloat16)
    out_grad = (gate_attn * hidden_total).astype(jnp.bfloat16).reshape(N_DP, TOK_DEV, HEADS, HEAD_DIM)

    def backward_shard(total, item):
        query_rows, mask_block, cite_row, grad_rows = item
        stored, keys, values, allowed = shard_tensors(image_kv, image_owner, cite_row, mask_block)
        query_wide = query_rows.astype(jnp.float32)
        probs = attention_probs(query_wide, keys, allowed)
        grad_wide = grad_rows.astype(jnp.float32)
        prob_grad = jnp.einsum('thd,khd->htk', grad_wide, values)
        score_grad = rounded(probs * (prob_grad - lax.optimization_barrier(jnp.sum(probs * prob_grad, axis=-1, keepdims=True))) * HEAD_DIM ** (-0.5))
        query_part = jnp.einsum('htk,khd->thd', score_grad, keys).astype(jnp.bfloat16).reshape(TOK_DEV, D)
        key_part = jnp.einsum('htk,thd->khd', score_grad, query_wide).astype(jnp.bfloat16).reshape(CITE, IT, D)
        value_part = jnp.einsum('htk,thd->khd', rounded(probs), grad_wide).astype(jnp.bfloat16).reshape(CITE, IT, D)
        parts = jnp.stack([key_part, value_part], axis=1).astype(jnp.float32)
        total = total.at[stored].add(parts)
        return (total, query_part)
    start = jnp.zeros((NI, 2, IT, D), jnp.float32)
    image_total, query_grad = lax.scan(backward_shard, start, (query_blocks, mask_blocks, citations, out_grad))
    query_grad = query_grad.reshape(TOKENS, D)
    image_kv_grad = image_total.astype(jnp.bfloat16)
    return (block_out, normed_out, hidden_grad, query_grad, image_kv_grad)
```

```python
import functools

import jax
import jax.numpy as jnp
from jax import lax
from jax.experimental import pallas as pl
from jax.experimental.pallas import tpu as pltpu
from jax.sharding import PartitionSpec as P

HEAD_DIM = 128
IT = 32
IMG_DEV = 2
TOK = 128
Y = 8
G = 4
EPS = 1e-05
MESH = pl.DeviceIdType.MESH
F32 = jnp.float32
BF16 = jnp.bfloat16
NT = (((1,), (1,)), ((), ()))
TN = (((0,), (0,)), ((), ()))
NN = (((1,), (0,)), ((), ()))


def dot(left, right, dims):
    return lax.dot_general(left, right, dims, preferred_element_type=F32)


def kernel(
    Z,
    M,
    cites,
    rows_ref,
    pos_ref,
    gate_ref,
    hidden_ref,
    query_ref,
    kv_ref,
    bias_ref,
    gain_ref,
    upstream_ref,
    block_ref,
    normed_ref,
    hgrad_ref,
    qgrad_ref,
    kvgrad_ref,
    kv_all,
    q_all,
    bias_all,
    hid,
    ups,
    ksel,
    vsel,
    probs,
    att_out,
    att_in,
    stat_out,
    stat_in,
    mixed,
    normed,
    hgrad,
    og_out,
    og_in,
    dq_out,
    cited,
    sib_out,
    sib_in,
    rs_out,
    rs_in,
    fin_out,
    kv_s,
    kv_r,
    q_s,
    q_r,
    b_s,
    b_r,
    ag_s,
    ag_r,
    sa_s,
    sa_r,
    att_s,
    att_r,
    st_s,
    st_r,
    og_s,
    og_r,
    dq_s,
    dq_r,
    sr_s,
    sr_r,
    rs_s,
    rs_r,
    fin_s,
    fin_r,
    loc,
):
    T = Z // 2
    n_rows = Z * Y * IMG_DEV
    width = G * HEAD_DIM
    feats = M * width
    dp = lax.axis_index("dp")
    mp = lax.axis_index("mp")
    z, y = dp // Y, dp % Y
    x, core = mp // 2, mp % 2
    a, b = y // G, y % G
    right = lax.rem(z + 1, Z) * Y + y
    left = lax.rem(z + Z - 1, Z) * Y + y
    sibling = (dp, x * 2 + 1 - core)
    in_group = a == core

    def peer(i):
        return (z * Y + core * G + i, x * 2 + a)

    barrier = pltpu.get_barrier_semaphore()
    for k in range(1, M):
        pl.semaphore_signal(
            barrier, inc=1, device_id=(dp, lax.rem(mp + k, M)), device_id_type=MESH
        )
    for other in (left, right):
        pl.semaphore_signal(barrier, inc=1, device_id=(other, mp), device_id_type=MESH)
    for k in range(1, G):
        pl.semaphore_signal(
            barrier, inc=1, device_id=peer(lax.rem(b + k, G)), device_id_type=MESH
        )

    @pl.when(jnp.logical_not(in_group))
    def _():
        pl.semaphore_signal(barrier, inc=1, device_id=peer(b), device_id_type=MESH)

    hid_copy = pltpu.make_async_copy(hidden_ref, hid, loc.at[0])
    ups_copy = pltpu.make_async_copy(upstream_ref, ups, loc.at[1])
    hid_copy.start()
    ups_copy.start()

    pl.semaphore_wait(barrier, (M - 1) + 2 + (G - 1) + jnp.where(in_group, 0, 1))

    def remote(src, dst, ssem, rsem, device):
        return pltpu.make_async_remote_copy(
            src_ref=src,
            dst_ref=dst,
            send_sem=ssem,
            recv_sem=rsem,
            device_id=device,
            device_id_type=MESH,
        )

    def give(i, src, dst_of, ssem, rsem):
        mine = in_group & (i == b)

        @pl.when(mine)
        def _():
            pltpu.make_async_copy(src, dst_of(b), rsem.at[b]).start()

        @pl.when(jnp.logical_not(mine))
        def _():
            remote(src, dst_of(b), ssem.at[i], rsem.at[b], peer(i)).start()

    def take(i, dst_of, ssem, rsem):
        mine = in_group & (i == b)

        @pl.when(mine)
        def _():
            pltpu.make_async_copy(dst_of(i), dst_of(i), rsem.at[i]).wait()

        @pl.when(jnp.logical_not(mine))
        def _():
            remote(dst_of(i), dst_of(i), ssem.at[i], rsem.at[i], peer(i)).wait_recv()

    def given(i, src, ssem, rsem):
        mine = in_group & (i == b)

        @pl.when(jnp.logical_not(mine))
        def _():
            remote(src, src, ssem.at[i], rsem.at[i], peer(i)).wait_send()

    def head(i):
        return pl.ds(pl.multiple_of(i * HEAD_DIM, HEAD_DIM), HEAD_DIM)

    def kv_src(i):
        return kv_ref.at[:, :, :, head(i)]

    def piece(zb, yy):
        return kv_all.at[pl.ds((zb * Y + yy) * IMG_DEV, IMG_DEV)]

    def kv_dst(i):
        return piece(z, core * G + i)

    def kv_dst_at_peer(i):
        return piece(z, y)

    for k in range(G):
        i = lax.rem(b + k, G)
        give(i, kv_src(i), kv_dst_at_peer, kv_s, kv_r)
    for k in range(G):
        i = lax.rem(b + k, G)
        give(i, query_ref.at[:, head(i)], lambda j: q_all.at[j], q_s, q_r)
        give(i, bias_ref, lambda j: bias_all.at[j], b_s, b_r)

    def ring_copy(way, t, zb, i):
        block = piece(zb, core * G + i)
        return remote(
            block, block, ag_s.at[way, t, i], ag_r.at[way, t, i], (right if way == 0 else left, mp)
        )

    def half_block(zb):
        return kv_all.at[pl.ds((zb * Y + core * G) * IMG_DEV, G * IMG_DEV)]

    def other_half_block(zb):
        return kv_all.at[pl.ds((zb * Y + (1 - core) * G) * IMG_DEV, G * IMG_DEV)]

    def to_sibling(n, zb):
        remote(half_block(zb), half_block(zb), sa_s.at[n], sa_r.at[n], sibling).start()

    def from_way(way, t):
        return lax.rem(z + (Z - t if way == 0 else t), Z)

    def in_step(way, t, i):
        return t < T or (i < G // 2) == (way == 0)

    for i in range(G):
        take(i, kv_dst, kv_s, kv_r)
        for way in (0, 1):
            if in_step(way, 1, i):
                ring_copy(way, 0, z, i).start()
    to_sibling(0, z)
    for t in range(1, T + 1):
        for i in range(G):
            for way in (0, 1):
                if in_step(way, t, i):
                    zb = from_way(way, t)
                    ring_copy(way, t - 1, zb, i).wait_recv()
                    if t < T and in_step(way, t + 1, i):
                        ring_copy(way, t, zb, i).start()
        if t < T:
            to_sibling(2 * t - 1, from_way(0, t))
            to_sibling(2 * t, from_way(1, t))
        else:
            to_sibling(2 * t - 1, from_way(0, t))
    for n in range(Z):
        zb = from_way(n % 2 ^ 1, (n + 1) // 2)
        remote(other_half_block(zb), other_half_block(zb), sa_s.at[n], sa_r.at[n], sibling).wait_recv()
    for i in range(G):
        take(i, lambda j: q_all.at[j], q_s, q_r)
        take(i, lambda j: bias_all.at[j], b_s, b_r)

    scale = HEAD_DIM**-0.5
    log2e = 1.4426950408889634

    def forward(s, _):
        for n in range(cites):
            row = rows_ref[s * cites + n]
            ksel[s, n * IT : (n + 1) * IT] = kv_all[row, 0]
            vsel[s, n * IT : (n + 1) * IT] = kv_all[row, 1]
        scores = dot(ksel[s], q_all[s], NT) * (scale * log2e)
        scores = scores.reshape(cites, IT, TOK) + bias_all[s][:, None, :]
        top = jnp.max(jnp.max(scores, axis=0), axis=0, keepdims=True)
        weights = jnp.exp2(scores - top[None])
        total = jnp.sum(jnp.sum(weights, axis=0), axis=0, keepdims=True)
        weights = (weights * (1.0 / total)[None]).reshape(cites * IT, TOK)
        probs[s] = weights
        att_out[s] = dot(weights.astype(BF16), vsel[s], TN).astype(BF16)
        give(s, att_out.at[s], lambda j: att_in.at[j], att_s, att_r)
        return 0

    lax.fori_loop(0, G, forward, 0)

    gate = gate_ref[0]
    hid_copy.wait()
    ups_copy.wait()
    gain = gain_ref[pl.ds(mp, 1), :]
    square = jnp.zeros((TOK, HEAD_DIM), F32)
    inner = jnp.zeros((TOK, HEAD_DIM), F32)
    for i in range(G):
        take(i, lambda j: att_in.at[j], att_s, att_r)
        lanes = slice(i * HEAD_DIM, (i + 1) * HEAD_DIM)
        block = (hid[:, lanes].astype(F32) + gate * att_in[i].astype(F32)).astype(BF16)
        mixed[:, lanes] = block
        wide = block.astype(F32)
        square += wide * wide
        inner += gain[:, lanes] * ups[:, lanes].astype(F32) * wide
    block_copy = pltpu.make_async_copy(mixed, block_ref, loc.at[2])
    block_copy.start()
    lane = lax.broadcasted_iota(jnp.int32, (TOK, HEAD_DIM), 1)
    both = jnp.where(
        lane == 0, jnp.sum(square, axis=1, keepdims=True), jnp.sum(inner, axis=1, keepdims=True)
    )
    stat_out[...] = jnp.transpose(both)[:8]
    stat_in[mp] = stat_out[...]
    for k in range(1, M):
        other = lax.rem(mp + k, M)
        remote(stat_out, stat_in.at[mp], st_s.at[k], st_r.at[mp], (dp, other)).start()
    for k in range(1, M):
        other = lax.rem(mp + k, M)
        remote(stat_out, stat_in.at[other], st_s.at[k], st_r.at[other], (dp, other)).wait_recv()
    total = stat_in[0]
    for k in range(1, M):
        total += stat_in[k]
    columns = jnp.transpose(jnp.concatenate([total] * (TOK // 8), axis=0))
    inverse = lax.rsqrt(columns[:, 0:1] / feats + EPS)
    slope = inverse * inverse * inverse * columns[:, 1:2] / feats
    for i in range(G):
        lanes = slice(i * HEAD_DIM, (i + 1) * HEAD_DIM)
        wide = mixed[:, lanes].astype(F32)
        weighted = gain[:, lanes] * ups[:, lanes].astype(F32)
        grad = inverse * weighted - wide * slope
        og_out[i] = (gate * grad).astype(BF16)
        give(i, og_out.at[i], lambda j: og_in.at[j], og_s, og_r)
        hgrad[:, lanes] = grad.astype(BF16)
        normed[:, lanes] = (wide * inverse * gain[:, lanes]).astype(BF16)
    normed_copy = pltpu.make_async_copy(normed, normed_ref, loc.at[3])
    hgrad_copy = pltpu.make_async_copy(hgrad, hgrad_ref, loc.at[4])
    normed_copy.start()
    hgrad_copy.start()

    def qgrad_slot(j):
        return qgrad_ref.at[:, head(j)]

    def backward(s, _):
        take(s, lambda j: og_in.at[j], og_s, og_r)
        out_grad = og_in[s]
        weights = probs[s]
        prob_grad = dot(vsel[s], out_grad, NT)
        mean = jnp.sum(weights * prob_grad, axis=0, keepdims=True)
        score_grad = (weights * (prob_grad - mean) * scale).astype(BF16)
        dq_out[s] = dot(score_grad, ksel[s], TN).astype(BF16)
        give(s, dq_out.at[s], qgrad_slot, dq_s, dq_r)
        cited[s, :cites, 0] = dot(score_grad, q_all[s], NN).reshape(cites, IT, HEAD_DIM)
        cited[s, :cites, 1] = dot(weights.astype(BF16), out_grad, NN).reshape(cites, IT, HEAD_DIM)
        cited[s, cites] = jnp.zeros((2, IT, HEAD_DIM), F32)
        return 0

    lax.fori_loop(0, G, backward, 0)

    def part(zb, yy, image):
        row = (zb * Y + yy) * IMG_DEV + image
        total = cited[0, pos_ref[row]]
        for s in range(1, G):
            total += cited[s, pos_ref[s * n_rows + row]]
        return total

    def target(way, t):
        return lax.rem(z + (T - t if way == 0 else Z - T + t), Z)

    order = [target(0, 0)]
    for t in range(1, T):
        order += [target(0, t), target(1, t)]
    order += [z]
    for n, zb in enumerate(order):

        def for_sibling(i, _):
            for image in range(IMG_DEV):
                sib_out[n, i, image] = part(zb, (1 - core) * G + i, image).astype(BF16)
            return 0

        lax.fori_loop(0, G, for_sibling, 0)
        remote(sib_out.at[n], sib_in.at[n], sr_s.at[n], sr_r.at[n], sibling).start()

    def pass_on(way, t, i):
        return remote(
            rs_out.at[way, t, i],
            rs_in.at[way, t, i],
            rs_s.at[way, t, i],
            rs_r.at[way, t, i],
            (right if way == 0 else left, mp),
        )

    def sib_wait(n):
        remote(sib_out.at[n], sib_in.at[n], sr_s.at[n], sr_r.at[n], sibling).wait_recv()

    half = G // 2
    for t in range(T):
        for n in (0,) if t == 0 else (2 * t - 1, 2 * t):
            sib_wait(n)
        for h in (0, 1):

            def step(i, _):
                for way in (0, 1):
                    if t == 0 and h != way:
                        continue
                    n = 0 if t == 0 else 2 * t - 1 + way
                    arrived = t > 1 or (t == 1 and h == way)
                    if arrived:
                        pass_on(way, t - 1, i).wait_recv()
                    for image in range(IMG_DEV):
                        value = part(target(way, t), core * G + i, image)
                        value += sib_in[n, i, image].astype(F32)
                        if arrived:
                            value += rs_in[way, t - 1, i, image].astype(F32)
                        rs_out[way, t, i, image] = value.astype(BF16)
                    pass_on(way, t, i).start()
                return 0

            lax.fori_loop(h * half, (h + 1) * half, step, 0)

    def kvgrad_slot(j):
        return kvgrad_ref.at[:, :, :, head(j)]

    sib_wait(Z - 1)

    def finish(i, _):
        for way in (0, 1):
            pass_on(way, T - 1, i).wait_recv()
        for image in range(IMG_DEV):
            value = part(z, core * G + i, image) + sib_in[Z - 1, i, image].astype(F32)
            value += rs_in[0, T - 1, i, image].astype(F32) + rs_in[1, T - 1, i, image].astype(F32)
            fin_out[i, image] = value.astype(BF16)
        give(i, fin_out.at[i], kvgrad_slot, fin_s, fin_r)
        return 0

    lax.fori_loop(0, G, finish, 0)

    for i in range(G):
        given(i, kv_src(i), kv_s, kv_r)
        given(i, query_ref.at[:, head(i)], q_s, q_r)
        given(i, bias_ref, b_s, b_r)
        given(i, att_out.at[i], att_s, att_r)
        given(i, og_out.at[i], og_s, og_r)
        given(i, dq_out.at[i], dq_s, dq_r)
        given(i, fin_out.at[i], fin_s, fin_r)
        for way in (0, 1):
            for t in range(T):
                if in_step(way, t + 1, i):
                    ring_copy(way, t, z, i).wait_send()
                if t > 0 or (i < half) == (way == 0):
                    pass_on(way, t, i).wait_send()
    for n in range(Z):
        remote(half_block(z), half_block(z), sa_s.at[n], sa_r.at[n], sibling).wait_send()
        remote(sib_out.at[n], sib_in.at[n], sr_s.at[n], sr_r.at[n], sibling).wait_send()
    for k in range(1, M):
        remote(stat_out, stat_in.at[0], st_s.at[k], st_r.at[0], (dp, lax.rem(mp + k, M))).wait_send()
    block_copy.wait()
    normed_copy.wait()
    hgrad_copy.wait()
    for i in range(G):
        take(i, qgrad_slot, dq_s, dq_r)
        take(i, kvgrad_slot, fin_s, fin_r)


def local(
    Z,
    M,
    hidden_in,
    queries,
    image_kv,
    image_owner,
    citations,
    cite_mask,
    gate_scalars,
    norm_gain,
    upstream,
):
    width = hidden_in.shape[1]
    cites = cite_mask.shape[1]
    n_rows = Z * Y * IMG_DEV
    dp = lax.axis_index("dp")
    mp = lax.axis_index("mp")
    first = dp // Y * Y + mp % 2 * G
    ids = jnp.arange(n_rows, dtype=jnp.int32)
    cited_ids = lax.dynamic_slice_in_dim(citations, first, G, 0)
    rows = jnp.sum(jnp.where(cited_ids[:, :, None] == ids, image_owner, 0), axis=-1)
    places = cites - jnp.arange(cites, dtype=jnp.int32)
    pos = cites - jnp.max(
        jnp.where(rows[:, :, None] == ids, places[None, :, None], 0), axis=1
    )
    bias = jnp.where(cite_mask > 0, 0.0, -1e30).astype(F32).T
    gate = jnp.tanh(gate_scalars)
    gain = norm_gain.reshape(M, width)

    T = Z // 2
    smem = pl.BlockSpec(memory_space=pltpu.SMEM)
    vmem = pl.BlockSpec(memory_space=pltpu.VMEM)
    anywhere = pl.BlockSpec(memory_space=pl.ANY)
    heads = (G, TOK, HEAD_DIM)
    piece = (IMG_DEV, 2, IT, HEAD_DIM)
    keys = cites * IT
    dma = pltpu.SemaphoreType.DMA
    like = lambda v: jax.ShapeDtypeStruct(v.shape, v.dtype)
    return pl.pallas_call(
        functools.partial(kernel, Z, M, cites),
        out_shape=(like(hidden_in),) * 4 + (like(image_kv),),
        in_specs=[smem, smem, smem, anywhere, anywhere, anywhere, anywhere, vmem, anywhere],
        out_specs=(anywhere,) * 5,
        scratch_shapes=[
            pltpu.VMEM((n_rows, 2, IT, HEAD_DIM), BF16),
            pltpu.VMEM(heads, BF16),
            pltpu.VMEM((G, cites, TOK), F32),
            pltpu.VMEM((TOK, width), BF16),
            pltpu.VMEM((TOK, width), BF16),
            pltpu.VMEM((G, keys, HEAD_DIM), BF16),
            pltpu.VMEM((G, keys, HEAD_DIM), BF16),
            pltpu.VMEM((G, keys, TOK), F32),
            pltpu.VMEM(heads, BF16),
            pltpu.VMEM(heads, BF16),
            pltpu.VMEM((8, TOK), F32),
            pltpu.VMEM((M, 8, TOK), F32),
            pltpu.VMEM((TOK, width), BF16),
            pltpu.VMEM((TOK, width), BF16),
            pltpu.VMEM((TOK, width), BF16),
            pltpu.VMEM(heads, BF16),
            pltpu.VMEM(heads, BF16),
            pltpu.VMEM(heads, BF16),
            pltpu.VMEM((G, cites + 1, 2, IT, HEAD_DIM), F32),
            pltpu.VMEM((Z, G) + piece, BF16),
            pltpu.VMEM((Z, G) + piece, BF16),
            pltpu.VMEM((2, T, G) + piece, BF16),
            pltpu.VMEM((2, T, G) + piece, BF16),
            pltpu.VMEM((G,) + piece, BF16),
            dma((G,)),
            dma((G,)),
            dma((G,)),
            dma((G,)),
            dma((G,)),
            dma((G,)),
            dma((2, T, G)),
            dma((2, T, G)),
            dma((Z,)),
            dma((Z,)),
            dma((G,)),
            dma((G,)),
            dma((M,)),
            dma((M,)),
            dma((G,)),
            dma((G,)),
            dma((G,)),
            dma((G,)),
            dma((Z,)),
            dma((Z,)),
            dma((2, T, G)),
            dma((2, T, G)),
            dma((G,)),
            dma((G,)),
            dma((5,)),
        ],
        compiler_params=pltpu.CompilerParams(
            collective_id=0, has_side_effects=True, vmem_limit_bytes=48 * 1024 * 1024
        ),
        name="attend",
    )(
        rows.reshape(-1),
        pos.reshape(-1),
        gate,
        hidden_in,
        queries,
        image_kv,
        bias,
        gain,
        upstream,
    )


def solution(mesh):
    Z = mesh.shape["dp"] // Y
    M = mesh.shape["mp"]
    placed = (
        P("dp", "mp"),
        P("dp", "mp"),
        P("dp", None, None, "mp"),
        P(),
        P(),
        P("dp", None),
        P(),
        P(),
        P("dp", "mp"),
    )
    return jax.shard_map(
        functools.partial(local, Z, M),
        mesh=mesh,
        in_specs=placed,
        out_specs=(
            P("dp", "mp"),
            P("dp", "mp"),
            P("dp", "mp"),
            P("dp", "mp"),
            P("dp", None, None, "mp"),
        ),
        check_vma=False,
    )
```

```python
import functools

import jax
import jax.numpy as jnp
from jax import lax
from jax.experimental import pallas as pl
from jax.experimental.pallas import tpu as pltpu
from jax.sharding import PartitionSpec as P

HEAD_DIM = 128
IT = 32
IMG_DEV = 2
TOK = 128
Y = 8
G = 4
EPS = 1e-05
VMEM_BYTES = 63 * 1024 * 1024
MESH = pl.DeviceIdType.MESH
F32 = jnp.float32
BF16 = jnp.bfloat16
NT = (((1,), (1,)), ((), ()))
TN = (((0,), (0,)), ((), ()))
NN = (((1,), (0,)), ((), ()))


def dot(left, right, dims):
    return lax.dot_general(left, right, dims, preferred_element_type=F32)


def kernel(
    Z,
    M,
    cites,
    hidden_ref,
    query_ref,
    kv_ref,
    owner_ref,
    citation_ref,
    mask_ref,
    gate_ref,
    gain_ref,
    upstream_ref,
    block_ref,
    normed_ref,
    hgrad_ref,
    qgrad_ref,
    kvgrad_ref,
    owner,
    citation,
    gate_in,
    gains,
    pos_make,
    pos,
    kv_all,
    q_all,
    mask_all,
    hid,
    ups,
    ksel,
    vsel,
    probs,
    att_out,
    att_in,
    stat_out,
    stat_in,
    mixed,
    normed,
    hgrad,
    og_out,
    og_in,
    dq_out,
    cited,
    sib_out,
    sib_in,
    rs_out,
    rs_in,
    fin_out,
    kv_s,
    kv_r,
    q_s,
    q_r,
    b_s,
    b_r,
    ag_s,
    ag_r,
    sa_s,
    sa_r,
    att_s,
    att_r,
    st_s,
    st_r,
    og_s,
    og_r,
    dq_s,
    dq_r,
    sr_s,
    sr_r,
    rs_s,
    rs_r,
    fin_s,
    fin_r,
    loc,
):
    T = Z // 2
    n_rows = Z * Y * IMG_DEV
    width = G * HEAD_DIM
    feats = M * width
    dp = lax.axis_index("dp")
    mp = lax.axis_index("mp")
    z, y = dp // Y, dp % Y
    x, core = mp // 2, mp % 2
    a, b = y // G, y % G
    right = lax.rem(z + 1, Z) * Y + y
    left = lax.rem(z + Z - 1, Z) * Y + y
    sibling = (dp, x * 2 + 1 - core)
    in_group = a == core

    def peer(i):
        return (z * Y + core * G + i, x * 2 + a)

    barrier = pltpu.get_barrier_semaphore()
    for k in range(1, M):
        pl.semaphore_signal(
            barrier, inc=1, device_id=(dp, lax.rem(mp + k, M)), device_id_type=MESH
        )
    for other in (left, right):
        pl.semaphore_signal(barrier, inc=1, device_id=(other, mp), device_id_type=MESH)
    for k in range(1, G):
        pl.semaphore_signal(
            barrier, inc=1, device_id=peer(lax.rem(b + k, G)), device_id_type=MESH
        )

    @pl.when(jnp.logical_not(in_group))
    def _():
        pl.semaphore_signal(barrier, inc=1, device_id=peer(b), device_id_type=MESH)

    own_copies = []
    for source, place in (
        (citation_ref, citation),
        (owner_ref, owner),
        (gate_ref, gate_in),
        (gain_ref, gains),
        (hidden_ref, hid),
        (upstream_ref, ups),
    ):
        copy = pltpu.make_async_copy(source, place, loc.at[len(own_copies)])
        copy.start()
        own_copies.append(copy)

    pl.semaphore_wait(barrier, (M - 1) + 2 + (G - 1) + jnp.where(in_group, 0, 1))

    def remote(src, dst, ssem, rsem, device):
        return pltpu.make_async_remote_copy(
            src_ref=src,
            dst_ref=dst,
            send_sem=ssem,
            recv_sem=rsem,
            device_id=device,
            device_id_type=MESH,
        )

    def give(i, src, dst_of, ssem, rsem):
        mine = in_group & (i == b)

        @pl.when(mine)
        def _():
            pltpu.make_async_copy(src, dst_of(b), rsem.at[b]).start()

        @pl.when(jnp.logical_not(mine))
        def _():
            remote(src, dst_of(b), ssem.at[i], rsem.at[b], peer(i)).start()

    def take(i, dst_of, ssem, rsem):
        mine = in_group & (i == b)

        @pl.when(mine)
        def _():
            pltpu.make_async_copy(dst_of(i), dst_of(i), rsem.at[i]).wait()

        @pl.when(jnp.logical_not(mine))
        def _():
            remote(dst_of(i), dst_of(i), ssem.at[i], rsem.at[i], peer(i)).wait_recv()

    def given(i, src, ssem, rsem):
        mine = in_group & (i == b)

        @pl.when(jnp.logical_not(mine))
        def _():
            remote(src, src, ssem.at[i], rsem.at[i], peer(i)).wait_send()

    def head(i):
        return pl.ds(pl.multiple_of(i * HEAD_DIM, HEAD_DIM), HEAD_DIM)

    def kv_src(i):
        return kv_ref.at[:, :, :, head(i)]

    def piece(zb, yy):
        return kv_all.at[pl.ds((zb * Y + yy) * IMG_DEV, IMG_DEV)]

    def kv_dst(i):
        return piece(z, core * G + i)

    def kv_dst_at_peer(i):
        return piece(z, y)

    for k in range(G):
        i = lax.rem(b + k, G)
        give(i, kv_src(i), kv_dst_at_peer, kv_s, kv_r)
    for k in range(G):
        i = lax.rem(b + k, G)
        give(i, query_ref.at[:, head(i)], lambda j: q_all.at[j], q_s, q_r)
        give(i, mask_ref, lambda j: mask_all.at[j], b_s, b_r)

    def ring_copy(way, t, zb, i):
        block = piece(zb, core * G + i)
        return remote(
            block, block, ag_s.at[way, t, i], ag_r.at[way, t, i], (right if way == 0 else left, mp)
        )

    def half_block(zb):
        return kv_all.at[pl.ds((zb * Y + core * G) * IMG_DEV, G * IMG_DEV)]

    def other_half_block(zb):
        return kv_all.at[pl.ds((zb * Y + (1 - core) * G) * IMG_DEV, G * IMG_DEV)]

    def to_sibling(n, zb):
        remote(half_block(zb), half_block(zb), sa_s.at[n], sa_r.at[n], sibling).start()

    def from_way(way, t):
        return lax.rem(z + (Z - t if way == 0 else t), Z)

    def in_step(way, t, i):
        return t < T or (i < G // 2) == (way == 0)

    for i in range(G):
        take(i, kv_dst, kv_s, kv_r)
        for way in (0, 1):
            if in_step(way, 1, i):
                ring_copy(way, 0, z, i).start()
    to_sibling(0, z)

    for copy in own_copies:
        copy.wait()
    first = z * Y + core * G

    def row_of(s, n):
        return owner[citation[n, first + s]]

    lanes = lax.broadcasted_iota(jnp.int32, (8, n_rows), 1)
    sublanes = lax.broadcasted_iota(jnp.int32, (8, n_rows), 0)

    def place(n, found):
        for s in range(G):
            found = jnp.where((sublanes == s) & (lanes == row_of(s, n)), n, found)
        return found

    pos_make[...] = lax.fori_loop(0, cites, place, jnp.full((8, n_rows), cites, jnp.int32))
    pos_copy = pltpu.make_async_copy(pos_make, pos, loc.at[9])
    pos_copy.start()

    for t in range(1, T + 1):
        for i in range(G):
            for way in (0, 1):
                if in_step(way, t, i):
                    zb = from_way(way, t)
                    ring_copy(way, t - 1, zb, i).wait_recv()
                    if t < T and in_step(way, t + 1, i):
                        ring_copy(way, t, zb, i).start()
        if t < T:
            to_sibling(2 * t - 1, from_way(0, t))
            to_sibling(2 * t, from_way(1, t))
        else:
            to_sibling(2 * t - 1, from_way(0, t))
    for n in range(Z):
        zb = from_way(n % 2 ^ 1, (n + 1) // 2)
        remote(other_half_block(zb), other_half_block(zb), sa_s.at[n], sa_r.at[n], sibling).wait_recv()
    for i in range(G):
        take(i, lambda j: q_all.at[j], q_s, q_r)
        take(i, lambda j: mask_all.at[j], b_s, b_r)

    scale = HEAD_DIM**-0.5
    log2e = 1.4426950408889634

    def forward(s, _):
        for n in range(cites):
            row = row_of(s, n)
            ksel[s, n * IT : (n + 1) * IT] = kv_all[row, 0]
            vsel[s, n * IT : (n + 1) * IT] = kv_all[row, 1]
        scores = dot(ksel[s], q_all[s], NT) * (scale * log2e)
        scores = scores.reshape(cites, IT, TOK)
        scores += jnp.where(mask_all[s] > 0, 0.0, -1e30).astype(F32)[:, None, :]
        top = jnp.max(jnp.max(scores, axis=0), axis=0, keepdims=True)
        weights = jnp.exp2(scores - top[None])
        total = jnp.sum(jnp.sum(weights, axis=0), axis=0, keepdims=True)
        weights = (weights * (1.0 / total)[None]).reshape(cites * IT, TOK)
        probs[s] = weights
        att_out[s] = dot(weights.astype(BF16), vsel[s], TN).astype(BF16)
        give(s, att_out.at[s], lambda j: att_in.at[j], att_s, att_r)
        return 0

    lax.fori_loop(0, G, forward, 0)

    gate = jnp.tanh(jnp.full((1, HEAD_DIM), gate_in[0], F32))
    gain = [gains[pl.ds(mp * G + i, 1), :] for i in range(G)]
    square = jnp.zeros((TOK, HEAD_DIM), F32)
    inner = jnp.zeros((TOK, HEAD_DIM), F32)
    for i in range(G):
        take(i, lambda j: att_in.at[j], att_s, att_r)
        lanes = slice(i * HEAD_DIM, (i + 1) * HEAD_DIM)
        block = (hid[:, lanes].astype(F32) + gate * att_in[i].astype(F32)).astype(BF16)
        mixed[:, lanes] = block
        wide = block.astype(F32)
        square += wide * wide
        inner += gain[i] * ups[:, lanes].astype(F32) * wide
    block_copy = pltpu.make_async_copy(mixed, block_ref, loc.at[6])
    block_copy.start()
    lane = lax.broadcasted_iota(jnp.int32, (TOK, HEAD_DIM), 1)
    both = jnp.where(
        lane == 0, jnp.sum(square, axis=1, keepdims=True), jnp.sum(inner, axis=1, keepdims=True)
    )
    stat_out[...] = jnp.transpose(both)[:8]
    stat_in[mp] = stat_out[...]
    for k in range(1, M):
        other = lax.rem(mp + k, M)
        remote(stat_out, stat_in.at[mp], st_s.at[k], st_r.at[mp], (dp, other)).start()
    for k in range(1, M):
        other = lax.rem(mp + k, M)
        remote(stat_out, stat_in.at[other], st_s.at[k], st_r.at[other], (dp, other)).wait_recv()
    total = stat_in[0]
    for k in range(1, M):
        total += stat_in[k]
    columns = jnp.transpose(jnp.concatenate([total] * (TOK // 8), axis=0))
    inverse = lax.rsqrt(columns[:, 0:1] / feats + EPS)
    slope = inverse * inverse * inverse * columns[:, 1:2] / feats
    for i in range(G):
        lanes = slice(i * HEAD_DIM, (i + 1) * HEAD_DIM)
        wide = mixed[:, lanes].astype(F32)
        weighted = gain[i] * ups[:, lanes].astype(F32)
        grad = inverse * weighted - wide * slope
        og_out[i] = (gate * grad).astype(BF16)
        give(i, og_out.at[i], lambda j: og_in.at[j], og_s, og_r)
        hgrad[:, lanes] = grad.astype(BF16)
        normed[:, lanes] = (wide * inverse * gain[i]).astype(BF16)
    normed_copy = pltpu.make_async_copy(normed, normed_ref, loc.at[7])
    hgrad_copy = pltpu.make_async_copy(hgrad, hgrad_ref, loc.at[8])
    normed_copy.start()
    hgrad_copy.start()

    def qgrad_slot(j):
        return qgrad_ref.at[:, head(j)]

    def backward(s, _):
        take(s, lambda j: og_in.at[j], og_s, og_r)
        out_grad = og_in[s]
        weights = probs[s]
        prob_grad = dot(vsel[s], out_grad, NT)
        mean = jnp.sum(weights * prob_grad, axis=0, keepdims=True)
        score_grad = (weights * (prob_grad - mean) * scale).astype(BF16)
        dq_out[s] = dot(score_grad, ksel[s], TN).astype(BF16)
        give(s, dq_out.at[s], qgrad_slot, dq_s, dq_r)
        cited[s, :cites, 0] = dot(score_grad, q_all[s], NN).reshape(cites, IT, HEAD_DIM)
        cited[s, :cites, 1] = dot(weights.astype(BF16), out_grad, NN).reshape(cites, IT, HEAD_DIM)
        cited[s, cites] = jnp.zeros((2, IT, HEAD_DIM), F32)
        return 0

    lax.fori_loop(0, G, backward, 0)

    def part(zb, yy, image):
        row = (zb * Y + yy) * IMG_DEV + image
        total = cited[0, pos[0, row]]
        for s in range(1, G):
            total += cited[s, pos[s, row]]
        return total

    def target(way, t):
        return lax.rem(z + (T - t if way == 0 else Z - T + t), Z)

    pos_copy.wait()
    order = [target(0, 0)]
    for t in range(1, T):
        order += [target(0, t), target(1, t)]
    order += [z]
    for n, zb in enumerate(order):

        def for_sibling(i, _):
            for image in range(IMG_DEV):
                sib_out[n, i, image] = part(zb, (1 - core) * G + i, image).astype(BF16)
            return 0

        lax.fori_loop(0, G, for_sibling, 0)
        remote(sib_out.at[n], sib_in.at[n], sr_s.at[n], sr_r.at[n], sibling).start()

    def pass_on(way, t, i):
        return remote(
            rs_out.at[way, t, i],
            rs_in.at[way, t, i],
            rs_s.at[way, t, i],
            rs_r.at[way, t, i],
            (right if way == 0 else left, mp),
        )

    def sib_wait(n):
        remote(sib_out.at[n], sib_in.at[n], sr_s.at[n], sr_r.at[n], sibling).wait_recv()

    half = G // 2
    for t in range(T):
        for n in (0,) if t == 0 else (2 * t - 1, 2 * t):
            sib_wait(n)
        for h in (0, 1):

            def step(i, _):
                for way in (0, 1):
                    if t == 0 and h != way:
                        continue
                    n = 0 if t == 0 else 2 * t - 1 + way
                    arrived = t > 1 or (t == 1 and h == way)
                    if arrived:
                        pass_on(way, t - 1, i).wait_recv()
                    for image in range(IMG_DEV):
                        value = part(target(way, t), core * G + i, image)
                        value += sib_in[n, i, image].astype(F32)
                        if arrived:
                            value += rs_in[way, t - 1, i, image].astype(F32)
                        rs_out[way, t, i, image] = value.astype(BF16)
                    pass_on(way, t, i).start()
                return 0

            lax.fori_loop(h * half, (h + 1) * half, step, 0)

    def kvgrad_slot(j):
        return kvgrad_ref.at[:, :, :, head(j)]

    sib_wait(Z - 1)

    def finish(i, _):
        for way in (0, 1):
            pass_on(way, T - 1, i).wait_recv()
        for image in range(IMG_DEV):
            value = part(z, core * G + i, image) + sib_in[Z - 1, i, image].astype(F32)
            value += rs_in[0, T - 1, i, image].astype(F32) + rs_in[1, T - 1, i, image].astype(F32)
            fin_out[i, image] = value.astype(BF16)
        give(i, fin_out.at[i], kvgrad_slot, fin_s, fin_r)
        return 0

    lax.fori_loop(0, G, finish, 0)

    for i in range(G):
        given(i, kv_src(i), kv_s, kv_r)
        given(i, query_ref.at[:, head(i)], q_s, q_r)
        given(i, mask_ref, b_s, b_r)
        given(i, att_out.at[i], att_s, att_r)
        given(i, og_out.at[i], og_s, og_r)
        given(i, dq_out.at[i], dq_s, dq_r)
        given(i, fin_out.at[i], fin_s, fin_r)
        for way in (0, 1):
            for t in range(T):
                if in_step(way, t + 1, i):
                    ring_copy(way, t, z, i).wait_send()
                if t > 0 or (i < half) == (way == 0):
                    pass_on(way, t, i).wait_send()
    for n in range(Z):
        remote(half_block(z), half_block(z), sa_s.at[n], sa_r.at[n], sibling).wait_send()
        remote(sib_out.at[n], sib_in.at[n], sr_s.at[n], sr_r.at[n], sibling).wait_send()
    for k in range(1, M):
        remote(stat_out, stat_in.at[0], st_s.at[k], st_r.at[0], (dp, lax.rem(mp + k, M))).wait_send()
    block_copy.wait()
    normed_copy.wait()
    hgrad_copy.wait()
    for i in range(G):
        take(i, qgrad_slot, dq_s, dq_r)
        take(i, kvgrad_slot, fin_s, fin_r)


def leave(*refs):
    sources, places, sems = refs[:5], refs[5:10], refs[10]
    copies = [pltpu.make_async_copy(s, p, sems.at[n]) for n, (s, p) in enumerate(zip(sources, places))]
    for copy in copies:
        copy.start()
    for copy in copies:
        copy.wait()


def local(
    Z,
    M,
    hidden_in,
    queries,
    image_kv,
    image_owner,
    citations,
    cite_mask,
    gate_scalars,
    norm_gain,
    upstream,
):
    width = hidden_in.shape[1]
    cites = cite_mask.shape[1]
    n_rows = Z * Y * IMG_DEV
    T = Z // 2
    hbm = pl.BlockSpec(memory_space=pltpu.HBM)
    heads = (G, TOK, HEAD_DIM)
    piece = (IMG_DEV, 2, IT, HEAD_DIM)
    keys = cites * IT
    dma = pltpu.SemaphoreType.DMA
    like = lambda v: jax.ShapeDtypeStruct(v.shape, v.dtype)
    results = pl.pallas_call(
        functools.partial(kernel, Z, M, cites),
        out_shape=(like(hidden_in),) * 4 + (like(image_kv),),
        in_specs=[hbm] * 9,
        out_specs=(hbm,) * 5,
        scratch_shapes=[
            pltpu.SMEM((n_rows,), jnp.int32),
            pltpu.SMEM(citations.shape[::-1], jnp.int32),
            pltpu.SMEM((1,), F32),
            pltpu.VMEM((M * G, HEAD_DIM), F32),
            pltpu.VMEM((8, n_rows), jnp.int32),
            pltpu.SMEM((8, n_rows), jnp.int32),
            pltpu.VMEM((n_rows, 2, IT, HEAD_DIM), BF16),
            pltpu.VMEM(heads, BF16),
            pltpu.VMEM((G, cites, TOK), jnp.int32),
            pltpu.VMEM((TOK, width), BF16),
            pltpu.VMEM((TOK, width), BF16),
            pltpu.VMEM((G, keys, HEAD_DIM), BF16),
            pltpu.VMEM((G, keys, HEAD_DIM), BF16),
            pltpu.VMEM((G, keys, TOK), F32),
            pltpu.VMEM(heads, BF16),
            pltpu.VMEM(heads, BF16),
            pltpu.VMEM((8, TOK), F32),
            pltpu.VMEM((M, 8, TOK), F32),
            pltpu.VMEM((TOK, width), BF16),
            pltpu.VMEM((TOK, width), BF16),
            pltpu.VMEM((TOK, width), BF16),
            pltpu.VMEM(heads, BF16),
            pltpu.VMEM(heads, BF16),
            pltpu.VMEM(heads, BF16),
            pltpu.VMEM((G, cites + 1, 2, IT, HEAD_DIM), F32),
            pltpu.VMEM((Z, G) + piece, BF16),
            pltpu.VMEM((Z, G) + piece, BF16),
            pltpu.VMEM((2, T, G) + piece, BF16),
            pltpu.VMEM((2, T, G) + piece, BF16),
            pltpu.VMEM((G,) + piece, BF16),
            dma((G,)),
            dma((G,)),
            dma((G,)),
            dma((G,)),
            dma((G,)),
            dma((G,)),
            dma((2, T, G)),
            dma((2, T, G)),
            dma((Z,)),
            dma((Z,)),
            dma((G,)),
            dma((G,)),
            dma((M,)),
            dma((M,)),
            dma((G,)),
            dma((G,)),
            dma((G,)),
            dma((G,)),
            dma((Z,)),
            dma((Z,)),
            dma((2, T, G)),
            dma((2, T, G)),
            dma((G,)),
            dma((G,)),
            dma((10,)),
        ],
        compiler_params=pltpu.CompilerParams(
            collective_id=0, has_side_effects=True, vmem_limit_bytes=VMEM_BYTES
        ),
        name="attend",
    )(
        hidden_in,
        queries,
        image_kv,
        image_owner,
        citations.T,
        cite_mask.T,
        gate_scalars,
        norm_gain.reshape(M * G, HEAD_DIM),
        upstream,
    )
    return pl.pallas_call(
        leave,
        out_shape=tuple(like(v) for v in results),
        in_specs=[hbm] * 5,
        out_specs=(hbm,) * 5,
        scratch_shapes=[dma((5,))],
        compiler_params=pltpu.CompilerParams(vmem_limit_bytes=VMEM_BYTES),
        name="leave",
    )(*results)


def solution(mesh):
    Z = mesh.shape["dp"] // Y
    M = mesh.shape["mp"]
    placed = (
        P("dp", "mp"),
        P("dp", "mp"),
        P("dp", None, None, "mp"),
        P(),
        P(),
        P("dp", None),
        P(),
        P(),
        P("dp", "mp"),
    )
    return jax.shard_map(
        functools.partial(local, Z, M),
        mesh=mesh,
        in_specs=placed,
        out_specs=(
            P("dp", "mp"),
            P("dp", "mp"),
            P("dp", "mp"),
            P("dp", "mp"),
            P("dp", None, None, "mp"),
        ),
        check_vma=False,
    )
```

```python
import functools

import jax
import jax.numpy as jnp
from jax import lax
from jax.experimental import pallas as pl
from jax.experimental.pallas import tpu as pltpu
from jax.sharding import PartitionSpec as P

HEAD_DIM = 128
IT = 32
IMG_DEV = 2
TOK = 128
Y = 8
G = 4
EPS = 1e-05
VMEM_BYTES = 63 * 1024 * 1024
MESH = pl.DeviceIdType.MESH
F32 = jnp.float32
BF16 = jnp.bfloat16
NT = (((1,), (1,)), ((), ()))
TN = (((0,), (0,)), ((), ()))
NN = (((1,), (0,)), ((), ()))


def dot(left, right, dims):
    return lax.dot_general(left, right, dims, preferred_element_type=F32)


def kernel(
    Z,
    M,
    cites,
    hidden_ref,
    query_ref,
    kv_ref,
    owner_ref,
    citation_ref,
    mask_ref,
    gate_ref,
    gain_ref,
    upstream_ref,
    block_ref,
    normed_ref,
    hgrad_ref,
    qgrad_ref,
    kvgrad_ref,
    owner,
    citation,
    gate_in,
    gains,
    pos_make,
    pos,
    k_all,
    v_all,
    q_all,
    hid_all,
    ups_all,
    mask_all,
    ksel,
    vsel,
    probs,
    plow,
    plow_t,
    block_out,
    normed_out,
    hgrad_out,
    dq_out,
    out_grad,
    stat_out,
    stat_y,
    stat_x,
    cited,
    sums,
    sib_out,
    sib_in,
    rs_out,
    rs_in,
    fin_out,
    sent,
    kv_r,
    token_r,
    ag_r,
    sa_r,
    stat_r,
    out_r,
    sr_r,
    rs_r,
    loc,
):
    T = Z // 2
    X = M // 2
    kv_all = (k_all, v_all)
    n_rows = Z * Y * IMG_DEV
    feats = M * G * HEAD_DIM
    dp = lax.axis_index("dp")
    mp = lax.axis_index("mp")
    z, y = dp // Y, dp % Y
    x, core = mp // 2, mp % 2
    a, b = y // G, y % G
    right = (lax.rem(z + 1, Z) * Y + y, mp)
    left = (lax.rem(z + Z - 1, Z) * Y + y, mp)
    sibling = (dp, x * 2 + 1 - core)
    in_group = a == core

    def peer(i):
        return (z * Y + core * G + i, x * 2 + a)

    def y_peer(k):
        return (z * Y + lax.rem(y + k, Y), mp)

    def x_peer(k):
        return (dp, lax.rem(x + k, X) * 2 + core)

    barrier = pltpu.get_barrier_semaphore()
    others = [peer(lax.rem(b + k, G)) for k in range(1, G)] + [right, left, sibling]
    others += [y_peer(k) for k in range(1, Y)] + [x_peer(k) for k in range(1, X)]
    for other in others:
        pl.semaphore_signal(barrier, inc=1, device_id=other, device_id_type=MESH)

    @pl.when(jnp.logical_not(in_group))
    def _():
        pl.semaphore_signal(barrier, inc=1, device_id=peer(b), device_id_type=MESH)

    own_copies = []
    for source, place in (
        (citation_ref, citation),
        (owner_ref, owner),
        (gate_ref, gate_in),
        (gain_ref, gains),
    ):
        copy = pltpu.make_async_copy(source, place, loc.at[len(own_copies)])
        copy.start()
        own_copies.append(copy)

    pl.semaphore_wait(barrier, len(others) + jnp.where(in_group, 0, 1))

    def remote(src, dst, ssem, rsem, device):
        return pltpu.make_async_remote_copy(
            src_ref=src,
            dst_ref=dst,
            send_sem=ssem,
            recv_sem=rsem,
            device_id=device,
            device_id_type=MESH,
        )

    GROUP, RING, PAIR, STAT, SUM_RING, SUM_PAIR = range(6)

    def give(i, src, dst, rsem):
        mine = in_group & (i == b)

        @pl.when(mine)
        def _():
            pltpu.make_async_copy(src, dst, rsem).start()

        @pl.when(jnp.logical_not(mine))
        def _():
            remote(src, dst, sent.at[GROUP], rsem, peer(i)).start()

    def landed(buffer, rsem):
        pltpu.make_async_copy(buffer, buffer, rsem).wait()

    def left_here(buffer, kind):
        pltpu.make_async_copy(buffer, buffer, sent.at[kind]).wait()

    def head(i):
        return pl.ds(pl.multiple_of(i * HEAD_DIM, HEAD_DIM), HEAD_DIM)

    def kv_src(kv, i):
        return kv_ref.at[:, kv, :, head(i)]

    def piece(kv, zb, yy):
        return kv_all[kv].at[pl.ds((zb * Y + yy) * IMG_DEV, IMG_DEV)]

    turn = [lax.rem(b + k, G) for k in range(G)]
    for kv in (0, 1):
        for i in turn:
            give(i, kv_src(kv, i), piece(kv, z, y), kv_r.at[kv, b // 2])

    half_rows = G * IMG_DEV // 2

    def half_share(kv, zb, h):
        return kv_all[kv].at[pl.ds((zb * Y + core * G) * IMG_DEV + h * half_rows, half_rows)]

    def ring_copy(way, kv, t, zb, h):
        block = half_share(kv, zb, h)
        return remote(
            block,
            block,
            sent.at[RING],
            ag_r.at[way, kv, t, h],
            right if way == 0 else left,
        )

    def share(kv, zb, which):
        return kv_all[kv].at[pl.ds((zb * Y + which * G) * IMG_DEV, G * IMG_DEV)]

    def to_sibling(kv, zb):
        block = share(kv, zb, core)
        remote(block, block, sent.at[PAIR], sa_r.at[kv], sibling).start()

    def from_sibling(kv):
        landed(kv_all[kv].at[pl.ds(0, n_rows // 2)], sa_r.at[kv])

    def from_way(way, t):
        return lax.rem(z + (Z - t if way == 0 else t), Z)

    def in_step(way, t, h):
        return t < T or h == way

    for kv in (0, 1):
        for h in (0, 1):
            landed(half_share(kv, z, h), kv_r.at[kv, h])
            for way in (0, 1):
                if in_step(way, 1, h):
                    ring_copy(way, kv, 0, z, h).start()
        to_sibling(kv, z)

    token_inputs = (query_ref, q_all), (hidden_ref, hid_all), (upstream_ref, ups_all)
    for i in turn:
        give(i, mask_ref, mask_all.at[b], token_r.at[0])
    for n, (source, place) in enumerate(token_inputs):
        for i in turn:
            give(i, source.at[:, head(i)], place.at[b], token_r.at[min(n, 1)])

    for copy in own_copies:
        copy.wait()
    first = z * Y + core * G

    def row_of(s, n):
        return owner[citation[n, first + s]]

    lanes = lax.broadcasted_iota(jnp.int32, (8, n_rows), 1)
    sublanes = lax.broadcasted_iota(jnp.int32, (8, n_rows), 0)

    def find(n, found):
        for s in range(G):
            found = jnp.where((sublanes == s) & (lanes == row_of(s, n)), n, found)
        return found

    pos_make[...] = lax.fori_loop(0, cites, find, jnp.full((8, n_rows), cites, jnp.int32))
    pos_copy = pltpu.make_async_copy(pos_make, pos, loc.at[4])
    pos_copy.start()

    def ring_step(kv, t):
        for h in (0, 1):
            for way in (0, 1):
                if in_step(way, t, h):
                    zb = from_way(way, t)
                    ring_copy(way, kv, t - 1, zb, h).wait_recv()
                    if t < T and in_step(way, t + 1, h):
                        ring_copy(way, kv, t, zb, h).start()
        to_sibling(kv, from_way(0, t))
        if t < T:
            to_sibling(kv, from_way(1, t))

    for t in range(1, T):
        ring_step(0, t)
        ring_step(1, t)
    ring_step(0, T)
    from_sibling(0)
    landed(probs.at[:, pl.ds(0, 96)], token_r.at[0])

    scale = HEAD_DIM**-0.5
    log2e = 1.4426950408889634

    def scores_of(s, _):
        for n in range(cites):
            ksel[s, n * IT : (n + 1) * IT] = k_all[row_of(s, n)]
        scores = dot(ksel[s], q_all[s], NT) * (scale * log2e)
        scores = scores.reshape(cites, IT, TOK)
        scores += jnp.where(mask_all[s] > 0, 0.0, -1e30).astype(F32)[:, None, :]
        top = jnp.max(jnp.max(scores, axis=0), axis=0, keepdims=True)
        weights = jnp.exp2(scores - top[None])
        total = jnp.sum(jnp.sum(weights, axis=0), axis=0, keepdims=True)
        weights = (weights * (1.0 / total)[None]).reshape(cites * IT, TOK)
        probs[s] = weights
        rounded = weights.astype(BF16)
        plow[s] = rounded
        plow_t[s] = rounded.T
        return 0

    lax.fori_loop(0, G, scores_of, 0)

    ring_step(1, T)
    from_sibling(1)
    landed(probs.at[:, pl.ds(0, 128)], token_r.at[1])

    gate = jnp.tanh(jnp.full((1, HEAD_DIM), gate_in[0], F32))
    gain = gains[pl.ds(x * Y + y, 1), :]
    stat_lane = lax.broadcasted_iota(jnp.int32, (TOK, HEAD_DIM), 1)

    def attend(s, stats):
        for n in range(cites):
            vsel[s, n * IT : (n + 1) * IT] = v_all[row_of(s, n)]
        attended = dot(plow_t[s], vsel[s], NN)
        block = (hid_all[s].astype(F32) + gate * attended).astype(BF16)
        block_out[s] = block
        wide = block.astype(F32)
        square = jnp.sum(wide * wide, axis=1, keepdims=True)
        inner = jnp.sum(gain * ups_all[s].astype(F32) * wide, axis=1, keepdims=True)
        stats = jnp.where(stat_lane == 2 * s, square, stats)
        return jnp.where(stat_lane == 2 * s + 1, inner, stats)

    stats = lax.fori_loop(0, G, attend, jnp.zeros((TOK, HEAD_DIM), F32))

    stat_out[0] = jnp.transpose(stats)[:8]
    stat_y[y] = stat_out[0]
    for k in range(1, Y):
        remote(stat_out.at[0], stat_y.at[y], sent.at[STAT], stat_r.at[0], y_peer(k)).start()
    for s in range(G):
        give(s, block_out.at[s], block_ref.at[:, head(b)], out_r.at[0])
    landed(stat_y.at[pl.ds(0, Y - 1)], stat_r.at[0])
    total = stat_y[0]
    for k in range(1, Y):
        total += stat_y[k]
    stat_out[1] = total
    stat_x[x] = total
    for k in range(1, X):
        remote(stat_out.at[1], stat_x.at[x], sent.at[STAT], stat_r.at[1], x_peer(k)).start()
    if X > 1:
        landed(stat_x.at[pl.ds(0, X - 1)], stat_r.at[1])
    total = stat_x[0]
    for k in range(1, X):
        total += stat_x[k]
    columns = jnp.transpose(jnp.concatenate([total] * (TOK // 8), axis=0))

    for s in range(G):
        inverse = lax.rsqrt(columns[:, 2 * s : 2 * s + 1] / feats + EPS)
        slope = inverse * inverse * inverse * columns[:, 2 * s + 1 : 2 * s + 2] / feats
        wide = block_out[s].astype(F32)
        grad = inverse * (gain * ups_all[s].astype(F32)) - wide * slope
        out_grad[s] = (gate * grad).astype(BF16)
        hgrad_out[s] = grad.astype(BF16)
        normed_out[s] = (wide * inverse * gain).astype(BF16)
        cited[1, s, :cites] = dot(plow[s], out_grad[s], NN).reshape(cites, IT, HEAD_DIM)
        for kv in (0, 1):
            cited[kv, s, cites] = jnp.zeros((IT, HEAD_DIM), F32)

    def part(kv, row):
        total = cited[kv, 0, pos[0, row]]
        for s in range(1, G):
            total += cited[kv, s, pos[s, row]]
        return total

    def target(way, t):
        return lax.rem(z + (T - t if way == 0 else Z - T + t), Z)

    order = [target(0, 0)]
    for t in range(1, T):
        order += [target(0, t), target(1, t)]
    order += [z]

    def for_sibling(kv):
        for n, zb in enumerate(order):
            base = (zb * Y + (1 - core) * G) * IMG_DEV
            for r in range(G * IMG_DEV):
                sib_out[kv, n, r] = part(kv, base + r).astype(BF16)
            remote(
                sib_out.at[kv, n],
                sib_in.at[kv, n],
                sent.at[SUM_PAIR],
                sr_r.at[kv, min(n, 1)],
                sibling,
            ).start()

    def pass_on(way, kv, t, h):
        return remote(
            rs_out.at[way, kv, t, h],
            rs_in.at[way, kv, t, h],
            sent.at[SUM_RING],
            rs_r.at[way, kv, t, h],
            right if way == 0 else left,
        )

    def own(kv, n, r):
        base = (order[n] * Y + core * G) * IMG_DEV
        return part(kv, base + r) + sib_in[kv, n, r].astype(F32)

    def sum_start(kv):
        landed(sib_in.at[kv, 0], sr_r.at[kv, 0])
        for way in (0, 1):
            for r in range(half_rows):
                rs_out[way, kv, 0, way, r] = own(kv, 0, way * half_rows + r).astype(BF16)
            pass_on(way, kv, 0, way).start()
        landed(sib_in.at[kv, pl.ds(1, Z - 1)], sr_r.at[kv, 1])
        for n in range(1, Z):
            for r in range(G * IMG_DEV):
                sums[kv, n - 1, r] = own(kv, n, r)

    def sum_step(kv, t):
        for j in (0, 1):
            for way in (0, 1):
                h = j ^ way ^ 1 if t == 1 else j
                arrived = t > 1 or h == way
                if arrived:
                    pass_on(way, kv, t - 1, h).wait_recv()
                for r in range(half_rows):
                    value = sums[kv, 2 * t - 2 + way, h * half_rows + r]
                    if arrived:
                        value += rs_in[way, kv, t - 1, h, r].astype(F32)
                    rs_out[way, kv, t, h, r] = value.astype(BF16)
                pass_on(way, kv, t, h).start()

    def sum_end(kv):
        for h in (0, 1):
            for way in (0, 1):
                pass_on(way, kv, T - 1, h).wait_recv()
            for r in range(half_rows):
                value = sums[kv, Z - 2, h * half_rows + r]
                for way in (0, 1):
                    value += rs_in[way, kv, T - 1, h, r].astype(F32)
                fin_out[kv, h * half_rows + r] = value.astype(BF16)
            for i in range(h * G // 2, (h + 1) * G // 2):
                piece_out = fin_out.at[kv, pl.ds(i * IMG_DEV, IMG_DEV)]
                give(i, piece_out, kvgrad_ref.at[:, kv, :, head(b)], out_r.at[0])

    pos_copy.wait()
    for_sibling(1)
    sum_start(1)
    for s in range(G):
        give(s, hgrad_out.at[s], hgrad_ref.at[:, head(b)], out_r.at[0])
        give(s, normed_out.at[s], normed_ref.at[:, head(b)], out_r.at[0])

    def backward(s, _):
        weights = probs[s]
        prob_grad = dot(vsel[s], out_grad[s], NT)
        mean = jnp.sum(weights * prob_grad, axis=0, keepdims=True)
        score_grad = (weights * (prob_grad - mean) * scale).astype(BF16)
        cited[0, s, :cites] = dot(score_grad, q_all[s], NN).reshape(cites, IT, HEAD_DIM)
        dq_out[s] = dot(score_grad, ksel[s], TN).astype(BF16)
        return 0

    lax.fori_loop(0, G // 2, backward, 0)
    sum_step(1, 1)
    lax.fori_loop(G // 2, G, backward, 0)

    for_sibling(0)
    if T > 2:
        sum_step(1, 2)
    sum_start(0)
    for t in range(3, T):
        sum_step(1, t)
    for s in range(G):
        give(s, dq_out.at[s], qgrad_ref.at[:, head(b)], out_r.at[0])
    sum_step(0, 1)
    sum_end(1)
    for t in range(2, T):
        sum_step(0, t)
    sum_end(0)

    left_here(sib_in.at[:, pl.ds(0, Z - 1)], RING)
    left_here(sib_in, PAIR)
    left_here(stat_y.at[pl.ds(0, Y - 1)], STAT)
    if X > 1:
        left_here(stat_x.at[pl.ds(0, X - 1)], STAT)
    left_here(sib_in.at[:, pl.ds(0, Z - 1)], SUM_RING)
    left_here(sib_in, SUM_PAIR)
    group_rows = 304 * 2

    @pl.when(in_group)
    def _():
        left_here(probs.at[pl.ds(0, G - 1), pl.ds(0, group_rows)], GROUP)

    @pl.when(jnp.logical_not(in_group))
    def _():
        left_here(probs.at[:, pl.ds(0, group_rows)], GROUP)

    landed(probs.at[:, pl.ds(0, 160 * 2)], out_r.at[0])


def leave(*refs):
    sources, places, stages, sems = refs[:5], refs[5:10], refs[10:15], refs[15]
    loads = [
        pltpu.make_async_copy(s, p, sems.at[0, n]) for n, (s, p) in enumerate(zip(sources, stages))
    ]
    stores = [
        pltpu.make_async_copy(s, p, sems.at[1, n]) for n, (s, p) in enumerate(zip(stages, places))
    ]
    for copy in loads:
        copy.start()
    for load, store in zip(loads, stores):
        load.wait()
        store.start()
    for copy in stores:
        copy.wait()


def local(
    Z,
    M,
    hidden_in,
    queries,
    image_kv,
    image_owner,
    citations,
    cite_mask,
    gate_scalars,
    norm_gain,
    upstream,
):
    cites = cite_mask.shape[1]
    n_rows = Z * Y * IMG_DEV
    T = Z // 2
    hbm = pl.BlockSpec(memory_space=pltpu.HBM)
    heads = (G, TOK, HEAD_DIM)
    share = (G * IMG_DEV, IT, HEAD_DIM)
    half = (G * IMG_DEV // 2, IT, HEAD_DIM)
    keys = cites * IT
    dma = pltpu.SemaphoreType.DMA
    like = lambda v: jax.ShapeDtypeStruct(v.shape, v.dtype)
    results = pl.pallas_call(
        functools.partial(kernel, Z, M, cites),
        out_shape=(like(hidden_in),) * 4 + (like(image_kv),),
        in_specs=[hbm] * 9,
        out_specs=(hbm,) * 5,
        scratch_shapes=[
            pltpu.SMEM((n_rows,), jnp.int32),
            pltpu.SMEM(citations.shape[::-1], jnp.int32),
            pltpu.SMEM((1,), F32),
            pltpu.VMEM((M * G, HEAD_DIM), F32),
            pltpu.VMEM((8, n_rows), jnp.int32),
            pltpu.SMEM((8, n_rows), jnp.int32),
            pltpu.VMEM((n_rows, IT, HEAD_DIM), BF16),
            pltpu.VMEM((n_rows, IT, HEAD_DIM), BF16),
            pltpu.VMEM(heads, BF16),
            pltpu.VMEM(heads, BF16),
            pltpu.VMEM(heads, BF16),
            pltpu.VMEM((G, cites, TOK), jnp.int32),
            pltpu.VMEM((G, keys, HEAD_DIM), BF16),
            pltpu.VMEM((G, keys, HEAD_DIM), BF16),
            pltpu.VMEM((G, keys, TOK), F32),
            pltpu.VMEM((G, keys, TOK), BF16),
            pltpu.VMEM((G, TOK, keys), BF16),
            pltpu.VMEM(heads, BF16),
            pltpu.VMEM(heads, BF16),
            pltpu.VMEM(heads, BF16),
            pltpu.VMEM(heads, BF16),
            pltpu.VMEM(heads, BF16),
            pltpu.VMEM((2, 8, TOK), F32),
            pltpu.VMEM((Y, 8, TOK), F32),
            pltpu.VMEM((M // 2, 8, TOK), F32),
            pltpu.VMEM((2, G, cites + 1, IT, HEAD_DIM), F32),
            pltpu.VMEM((2, Z - 1) + share, F32),
            pltpu.VMEM((2, Z) + share, BF16),
            pltpu.VMEM((2, Z) + share, BF16),
            pltpu.VMEM((2, 2, T, 2) + half, BF16),
            pltpu.VMEM((2, 2, T, 2) + half, BF16),
            pltpu.VMEM((2,) + share, BF16),
            dma((6,)),
            dma((2, 2)),
            dma((2,)),
            dma((2, 2, T, 2)),
            dma((2,)),
            dma((2,)),
            dma((1,)),
            dma((2, 2)),
            dma((2, 2, T, 2)),
            dma((5,)),
        ],
        compiler_params=pltpu.CompilerParams(
            collective_id=0, has_side_effects=True, vmem_limit_bytes=VMEM_BYTES
        ),
        name="attend",
    )(
        hidden_in,
        queries,
        image_kv,
        image_owner,
        citations.T,
        cite_mask.T,
        gate_scalars,
        norm_gain.reshape(M * G, HEAD_DIM),
        upstream,
    )
    return pl.pallas_call(
        leave,
        out_shape=tuple(like(v) for v in results),
        in_specs=[hbm] * 5,
        out_specs=(hbm,) * 5,
        scratch_shapes=[pltpu.VMEM(v.shape, v.dtype) for v in results] + [dma((2, 5))],
        compiler_params=pltpu.CompilerParams(vmem_limit_bytes=VMEM_BYTES),
        name="leave",
    )(*results)


def solution(mesh):
    Z = mesh.shape["dp"] // Y
    M = mesh.shape["mp"]
    placed = (
        P("dp", "mp"),
        P("dp", "mp"),
        P("dp", None, None, "mp"),
        P(),
        P(),
        P("dp", None),
        P(),
        P(),
        P("dp", "mp"),
    )
    return jax.shard_map(
        functools.partial(local, Z, M),
        mesh=mesh,
        in_specs=placed,
        out_specs=(
            P("dp", "mp"),
            P("dp", "mp"),
            P("dp", "mp"),
            P("dp", "mp"),
            P("dp", None, None, "mp"),
        ),
        check_vma=False,
    )
```

```python
import functools

import jax
import jax.numpy as jnp
from jax import lax
from jax.experimental import pallas as pl
from jax.experimental.pallas import tpu as pltpu
from jax.sharding import PartitionSpec as P

HEAD_DIM = 128
IT = 32
IMG_DEV = 2
TOK = 128
Y = 8
G = 4
EPS = 1e-05
VMEM_BYTES = 63 * 1024 * 1024
MESH = pl.DeviceIdType.MESH
F32 = jnp.float32
BF16 = jnp.bfloat16
NT = (((1,), (1,)), ((), ()))
TN = (((0,), (0,)), ((), ()))
NN = (((1,), (0,)), ((), ()))


def dot(left, right, dims):
    return lax.dot_general(left, right, dims, preferred_element_type=F32)


def kernel(
    Z,
    M,
    cites,
    hidden_ref,
    query_ref,
    kv_ref,
    owner_ref,
    citation_ref,
    mask_ref,
    gate_ref,
    gain_ref,
    upstream_ref,
    block_ref,
    normed_ref,
    hgrad_ref,
    qgrad_ref,
    kvgrad_ref,
    owner,
    citation,
    gate_in,
    gains,
    pos_make,
    pos,
    k_all,
    v_all,
    q_all,
    hid_all,
    ups_all,
    mask_all,
    ksel,
    vsel,
    probs,
    plow,
    plow_t,
    block_out,
    normed_out,
    hgrad_out,
    dq_out,
    out_grad,
    stat_out,
    stat_in,
    score_grad,
    dense_k,
    dense_v,
    sums,
    sib_out,
    sib_in,
    rs_out,
    rs_in,
    fin_out,
    sent,
    kv_r,
    token_r,
    ag_r,
    sa_r,
    stat_r,
    out_r,
    sr_r,
    rs_r,
    loc,
):
    T = Z // 2
    X = M // 2
    kv_all = (k_all, v_all)
    n_rows = Z * Y * IMG_DEV
    feats = M * G * HEAD_DIM
    dp = lax.axis_index("dp")
    mp = lax.axis_index("mp")
    z, y = dp // Y, dp % Y
    x, core = mp // 2, mp % 2
    a, b = y // G, y % G
    right = (lax.rem(z + 1, Z) * Y + y, mp)
    left = (lax.rem(z + Z - 1, Z) * Y + y, mp)
    sibling = (dp, x * 2 + 1 - core)
    in_group = a == core

    def peer(i):
        return (z * Y + core * G + i, x * 2 + a)

    far_first = sorted(range(1, X * Y), key=lambda k: -min(k % Y, Y - k % Y) - min(k // Y, X - k // Y))
    head_peers = [
        (z * Y + lax.rem(y + k % Y, Y), lax.rem(x + k // Y, X) * 2 + core) for k in far_first
    ]

    barrier = pltpu.get_barrier_semaphore()
    others = [peer(lax.rem(b + k, G)) for k in range(1, G)] + [right, left, sibling]
    others += head_peers
    for other in others:
        pl.semaphore_signal(barrier, inc=1, device_id=other, device_id_type=MESH)

    @pl.when(jnp.logical_not(in_group))
    def _():
        pl.semaphore_signal(barrier, inc=1, device_id=peer(b), device_id_type=MESH)

    own_copies = []
    for source, place in (
        (citation_ref, citation),
        (owner_ref, owner),
        (gate_ref, gate_in),
        (gain_ref, gains),
    ):
        copy = pltpu.make_async_copy(source, place, loc.at[len(own_copies)])
        copy.start()
        own_copies.append(copy)

    pl.semaphore_wait(barrier, len(others) + jnp.where(in_group, 0, 1))

    def remote(src, dst, ssem, rsem, device):
        return pltpu.make_async_remote_copy(
            src_ref=src,
            dst_ref=dst,
            send_sem=ssem,
            recv_sem=rsem,
            device_id=device,
            device_id_type=MESH,
        )

    GROUP, RING, PAIR, STAT, SUM_RING, SUM_PAIR = range(6)

    def give(i, src, dst, rsem):
        mine = in_group & (i == b)

        @pl.when(mine)
        def _():
            pltpu.make_async_copy(src, dst, rsem).start()

        @pl.when(jnp.logical_not(mine))
        def _():
            remote(src, dst, sent.at[GROUP], rsem, peer(i)).start()

    def landed(buffer, rsem):
        pltpu.make_async_copy(buffer, buffer, rsem).wait()

    def left_here(buffer, kind):
        pltpu.make_async_copy(buffer, buffer, sent.at[kind]).wait()

    def head(i):
        return pl.ds(pl.multiple_of(i * HEAD_DIM, HEAD_DIM), HEAD_DIM)

    def kv_src(kv, i):
        return kv_ref.at[:, kv, :, head(i)]

    def piece(kv, zb, yy):
        return kv_all[kv].at[pl.ds((zb * Y + yy) * IMG_DEV, IMG_DEV)]

    turn = [lax.rem(b + k, G) for k in range(G)]
    for kv in (0, 1):
        for i in turn:
            give(i, kv_src(kv, i), piece(kv, z, y), kv_r.at[kv, b // 2])

    half_rows = G * IMG_DEV // 2

    def half_share(kv, zb, h):
        return kv_all[kv].at[pl.ds((zb * Y + core * G) * IMG_DEV + h * half_rows, half_rows)]

    def ring_copy(way, kv, t, zb, h):
        block = half_share(kv, zb, h)
        return remote(
            block,
            block,
            sent.at[RING],
            ag_r.at[way, kv, t, h],
            right if way == 0 else left,
        )

    def share(kv, zb, which):
        return kv_all[kv].at[pl.ds((zb * Y + which * G) * IMG_DEV, G * IMG_DEV)]

    def to_sibling(kv, zb):
        block = share(kv, zb, core)
        remote(block, block, sent.at[PAIR], sa_r.at[kv], sibling).start()

    def from_sibling(kv):
        landed(kv_all[kv].at[pl.ds(0, n_rows // 2)], sa_r.at[kv])

    def from_way(way, t):
        return lax.rem(z + (Z - t if way == 0 else t), Z)

    def in_step(way, t, h):
        return t < T or h == way

    for kv in (0, 1):
        for h in (0, 1):
            landed(half_share(kv, z, h), kv_r.at[kv, h])
            for way in (0, 1):
                if in_step(way, 1, h):
                    ring_copy(way, kv, 0, z, h).start()
        to_sibling(kv, z)

    token_inputs = (query_ref, q_all), (hidden_ref, hid_all), (upstream_ref, ups_all)
    for i in turn:
        give(i, mask_ref, mask_all.at[b], token_r.at[0])
    for n, (source, place) in enumerate(token_inputs):
        for i in turn:
            give(i, source.at[:, head(i)], place.at[b], token_r.at[min(n, 1)])

    for copy in own_copies:
        copy.wait()
    first = z * Y + core * G

    def row_of(s, n):
        return owner[citation[n, first + s]]

    lanes = lax.broadcasted_iota(jnp.int32, (8, n_rows), 1)
    sublanes = lax.broadcasted_iota(jnp.int32, (8, n_rows), 0)

    def find(n, found):
        for s in range(G):
            found = jnp.where((sublanes == s) & (lanes == row_of(s, n)), n, found)
        return found

    pos_make[...] = lax.fori_loop(0, cites, find, jnp.full((8, n_rows), cites, jnp.int32))
    pos_copy = pltpu.make_async_copy(pos_make, pos, loc.at[4])
    pos_copy.start()

    def ring_step(kv, t):
        for h in (0, 1):
            for way in (0, 1):
                if in_step(way, t, h):
                    zb = from_way(way, t)
                    ring_copy(way, kv, t - 1, zb, h).wait_recv()
                    if t < T and in_step(way, t + 1, h):
                        ring_copy(way, kv, t, zb, h).start()
        to_sibling(kv, from_way(0, t))
        if t < T:
            to_sibling(kv, from_way(1, t))

    for t in range(1, T):
        ring_step(0, t)
        ring_step(1, t)
    ring_step(0, T)
    from_sibling(0)
    landed(probs.at[:, pl.ds(0, 96)], token_r.at[0])

    scale = HEAD_DIM**-0.5
    log2e = 1.4426950408889634

    def scores_of(s, _):
        for n in range(cites):
            ksel[s, n * IT : (n + 1) * IT] = k_all[row_of(s, n)]
        scores = dot(ksel[s], q_all[s], NT) * (scale * log2e)
        scores = scores.reshape(cites, IT, TOK)
        scores += jnp.where(mask_all[s] > 0, 0.0, -1e30).astype(F32)[:, None, :]
        top = jnp.max(jnp.max(scores, axis=0), axis=0, keepdims=True)
        weights = jnp.exp2(scores - top[None])
        total = jnp.sum(jnp.sum(weights, axis=0), axis=0, keepdims=True)
        weights = (weights * (1.0 / total)[None]).reshape(cites * IT, TOK)
        probs[s] = weights
        rounded = weights.astype(BF16)
        plow[s, :cites] = rounded.reshape(cites, IT, TOK)
        plow[s, cites] = jnp.zeros((IT, TOK), BF16)
        plow_t[s] = rounded.T
        return 0

    lax.fori_loop(0, G, scores_of, 0, unroll=True)

    ring_step(1, T)
    from_sibling(1)
    landed(probs.at[:, pl.ds(0, 128)], token_r.at[1])

    gate = jnp.tanh(jnp.full((1, HEAD_DIM), gate_in[0], F32))
    gain = gains[pl.ds(x * Y + y, 1), :]
    stat_lane = lax.broadcasted_iota(jnp.int32, (TOK, HEAD_DIM), 1)

    def attend(s, stats):
        for n in range(cites):
            vsel[s, n * IT : (n + 1) * IT] = v_all[row_of(s, n)]
        attended = dot(plow_t[s], vsel[s], NN)
        block = (hid_all[s].astype(F32) + gate * attended).astype(BF16)
        block_out[s] = block
        wide = block.astype(F32)
        square = jnp.sum(wide * wide, axis=1, keepdims=True)
        inner = jnp.sum(gain * ups_all[s].astype(F32) * wide, axis=1, keepdims=True)
        stats = jnp.where(stat_lane == 2 * s, square, stats)
        return jnp.where(stat_lane == 2 * s + 1, inner, stats)

    stats = lax.fori_loop(0, G, attend, jnp.zeros((TOK, HEAD_DIM), F32), unroll=True)

    stat_out[...] = jnp.transpose(stats)[:8]
    slot = x * Y + y
    stat_in[slot] = stat_out[...]
    for other in head_peers:
        remote(stat_out, stat_in.at[slot], sent.at[STAT], stat_r.at[0], other).start()
    for s in range(G):
        give(s, block_out.at[s], block_ref.at[:, head(b)], out_r.at[0])

    def order(n):
        return lax.rem(z + T + Z + (-((n + 1) // 2) if n % 2 else n // 2), Z)

    def spread(dense, source, which, n):
        base = (order(n) * Y + (core if which else 1 - core) * G) * IMG_DEV
        for r in range(G * IMG_DEV):
            for s in range(G):
                block = source[s, pos[s, base + r]]
                dense[which, n, r * IT : (r + 1) * IT, s * TOK : (s + 1) * TOK] = block

    pos_copy.wait()
    for n in range(Z):
        for which in (0, 1):
            spread(dense_v, plow, which, n)
    landed(stat_in.at[pl.ds(0, X * Y - 1)], stat_r.at[0])
    total = jnp.sum(stat_in[...], axis=0)
    columns = jnp.transpose(jnp.concatenate([total] * (TOK // 8), axis=0))

    for s in range(G):
        inverse = lax.rsqrt(columns[:, 2 * s : 2 * s + 1] / feats + EPS)
        slope = inverse * inverse * inverse * columns[:, 2 * s + 1 : 2 * s + 2] / feats
        wide = block_out[s].astype(F32)
        grad = inverse * (gain * ups_all[s].astype(F32)) - wide * slope
        out_grad[s] = (gate * grad).astype(BF16)
        hgrad_out[s] = grad.astype(BF16)
        normed_out[s] = (wide * inverse * gain).astype(BF16)

    def dense_sum(kv, which, n):
        tokens = (q_all, out_grad)[kv][...].reshape(G * TOK, HEAD_DIM)
        left_side = (dense_k, dense_v)[kv][which, n]
        return dot(left_side, tokens, NN).reshape(G * IMG_DEV, IT, HEAD_DIM)

    def for_sibling(kv):
        for n in range(Z):
            if kv == 0:
                spread(dense_k, score_grad, 0, n)
            sib_out[kv, n] = dense_sum(kv, 0, n).astype(BF16)
            remote(
                sib_out.at[kv, n],
                sib_in.at[kv, n],
                sent.at[SUM_PAIR],
                sr_r.at[kv, min(n, 1)],
                sibling,
            ).start()

    def pass_on(way, kv, t, h):
        return remote(
            rs_out.at[way, kv, t, h],
            rs_in.at[way, kv, t, h],
            sent.at[SUM_RING],
            rs_r.at[way, kv, t, h],
            right if way == 0 else left,
        )

    def sum_start(kv):
        if kv == 0:
            spread(dense_k, score_grad, 1, 0)
        value = dense_sum(kv, 1, 0)
        landed(sib_in.at[kv, 0], sr_r.at[kv, 0])
        value = (value + sib_in[kv, 0].astype(F32)).astype(BF16)
        for way in (0, 1):
            rs_out[way, kv, 0, way] = value[way * half_rows : (way + 1) * half_rows]
            pass_on(way, kv, 0, way).start()

    def sum_own(kv):
        landed(sib_in.at[kv, pl.ds(1, Z - 1)], sr_r.at[kv, 1])
        for n in range(1, Z):
            if kv == 0:
                spread(dense_k, score_grad, 1, n)
            sums[kv, n - 1] = dense_sum(kv, 1, n) + sib_in[kv, n].astype(F32)

    def sum_step(kv, t):
        for j in (0, 1):
            for way in (0, 1):
                h = j ^ way ^ 1 if t == 1 else j
                arrived = t > 1 or h == way
                if arrived:
                    pass_on(way, kv, t - 1, h).wait_recv()
                for r in range(half_rows):
                    value = sums[kv, 2 * t - 2 + way, h * half_rows + r]
                    if arrived:
                        value += rs_in[way, kv, t - 1, h, r].astype(F32)
                    rs_out[way, kv, t, h, r] = value.astype(BF16)
                pass_on(way, kv, t, h).start()

    def sum_end(kv):
        for h in (0, 1):
            for way in (0, 1):
                pass_on(way, kv, T - 1, h).wait_recv()
            for r in range(half_rows):
                value = sums[kv, Z - 2, h * half_rows + r]
                for way in (0, 1):
                    value += rs_in[way, kv, T - 1, h, r].astype(F32)
                fin_out[kv, h * half_rows + r] = value.astype(BF16)
            for i in range(h * G // 2, (h + 1) * G // 2):
                piece_out = fin_out.at[kv, pl.ds(i * IMG_DEV, IMG_DEV)]
                give(i, piece_out, kvgrad_ref.at[:, kv, :, head(b)], out_r.at[0])

    for_sibling(1)

    def backward(s, _):
        weights = probs[s]
        prob_grad = dot(vsel[s], out_grad[s], NT)
        mean = jnp.sum(weights * prob_grad, axis=0, keepdims=True)
        grad = (weights * (prob_grad - mean) * scale).astype(BF16)
        score_grad[s, :cites] = grad.reshape(cites, IT, TOK)
        score_grad[s, cites] = jnp.zeros((IT, TOK), BF16)
        return 0

    lax.fori_loop(0, G, backward, 0, unroll=True)
    sum_start(1)

    for_sibling(0)
    sum_start(0)
    sum_own(1)
    for s in range(G):
        give(s, hgrad_out.at[s], hgrad_ref.at[:, head(b)], out_r.at[0])
        give(s, normed_out.at[s], normed_ref.at[:, head(b)], out_r.at[0])
    sum_step(1, 1)
    sum_own(0)
    sum_step(0, 1)
    for s in range(G):
        grad = score_grad[s, :cites].reshape(cites * IT, TOK)
        dq_out[s] = dot(grad, ksel[s], TN).astype(BF16)
        give(s, dq_out.at[s], qgrad_ref.at[:, head(b)], out_r.at[0])
    for t in range(2, T):
        sum_step(1, t)
        sum_step(0, t)
    sum_end(1)
    sum_end(0)

    left_here(sib_in.at[:, pl.ds(0, Z - 1)], RING)
    left_here(sib_in, PAIR)
    left_here(stat_in.at[pl.ds(0, X * Y - 1)], STAT)
    left_here(sib_in.at[:, pl.ds(0, Z - 1)], SUM_RING)
    left_here(sib_in, SUM_PAIR)
    group_rows = 304 * 2

    @pl.when(in_group)
    def _():
        left_here(probs.at[pl.ds(0, G - 1), pl.ds(0, group_rows)], GROUP)

    @pl.when(jnp.logical_not(in_group))
    def _():
        left_here(probs.at[:, pl.ds(0, group_rows)], GROUP)

    landed(probs.at[:, pl.ds(0, 160 * 2)], out_r.at[0])


def leave(*refs):
    sources, places, stages, sems = refs[:5], refs[5:10], refs[10:15], refs[15]
    loads = [
        pltpu.make_async_copy(s, p, sems.at[0, n]) for n, (s, p) in enumerate(zip(sources, stages))
    ]
    stores = [
        pltpu.make_async_copy(s, p, sems.at[1, n]) for n, (s, p) in enumerate(zip(stages, places))
    ]
    for copy in loads:
        copy.start()
    for load, store in zip(loads, stores):
        load.wait()
        store.start()
    for copy in stores:
        copy.wait()


def local(
    Z,
    M,
    hidden_in,
    queries,
    image_kv,
    image_owner,
    citations,
    cite_mask,
    gate_scalars,
    norm_gain,
    upstream,
):
    cites = cite_mask.shape[1]
    n_rows = Z * Y * IMG_DEV
    T = Z // 2
    hbm = pl.BlockSpec(memory_space=pltpu.HBM)
    heads = (G, TOK, HEAD_DIM)
    share = (G * IMG_DEV, IT, HEAD_DIM)
    half = (G * IMG_DEV // 2, IT, HEAD_DIM)
    keys = cites * IT
    dma = pltpu.SemaphoreType.DMA
    like = lambda v: jax.ShapeDtypeStruct(v.shape, v.dtype)
    results = pl.pallas_call(
        functools.partial(kernel, Z, M, cites),
        out_shape=(like(hidden_in),) * 4 + (like(image_kv),),
        in_specs=[hbm] * 9,
        out_specs=(hbm,) * 5,
        scratch_shapes=[
            pltpu.SMEM((n_rows,), jnp.int32),
            pltpu.SMEM(citations.shape[::-1], jnp.int32),
            pltpu.SMEM((1,), F32),
            pltpu.VMEM((M * G, HEAD_DIM), F32),
            pltpu.VMEM((8, n_rows), jnp.int32),
            pltpu.SMEM((8, n_rows), jnp.int32),
            pltpu.VMEM((n_rows, IT, HEAD_DIM), BF16),
            pltpu.VMEM((n_rows, IT, HEAD_DIM), BF16),
            pltpu.VMEM(heads, BF16),
            pltpu.VMEM(heads, BF16),
            pltpu.VMEM(heads, BF16),
            pltpu.VMEM((G, cites, TOK), jnp.int32),
            pltpu.VMEM((G, keys, HEAD_DIM), BF16),
            pltpu.VMEM((G, keys, HEAD_DIM), BF16),
            pltpu.VMEM((G, keys, TOK), F32),
            pltpu.VMEM((G, cites + 1, IT, TOK), BF16),
            pltpu.VMEM((G, TOK, keys), BF16),
            pltpu.VMEM(heads, BF16),
            pltpu.VMEM(heads, BF16),
            pltpu.VMEM(heads, BF16),
            pltpu.VMEM(heads, BF16),
            pltpu.VMEM(heads, BF16),
            pltpu.VMEM((8, TOK), F32),
            pltpu.VMEM((M // 2 * Y, 8, TOK), F32),
            pltpu.VMEM((G, cites + 1, IT, TOK), BF16),
            pltpu.VMEM((2, Z, G * IMG_DEV * IT, G * TOK), BF16),
            pltpu.VMEM((2, Z, G * IMG_DEV * IT, G * TOK), BF16),
            pltpu.VMEM((2, Z - 1) + share, F32),
            pltpu.VMEM((2, Z) + share, BF16),
            pltpu.VMEM((2, Z) + share, BF16),
            pltpu.VMEM((2, 2, T, 2) + half, BF16),
            pltpu.VMEM((2, 2, T, 2) + half, BF16),
            pltpu.VMEM((2,) + share, BF16),
            dma((6,)),
            dma((2, 2)),
            dma((2,)),
            dma((2, 2, T, 2)),
            dma((2,)),
            dma((1,)),
            dma((1,)),
            dma((2, 2)),
            dma((2, 2, T, 2)),
            dma((5,)),
        ],
        compiler_params=pltpu.CompilerParams(
            collective_id=0, has_side_effects=True, vmem_limit_bytes=VMEM_BYTES
        ),
        name="attend",
    )(
        hidden_in,
        queries,
        image_kv,
        image_owner,
        citations.T,
        cite_mask.T,
        gate_scalars,
        norm_gain.reshape(M * G, HEAD_DIM),
        upstream,
    )
    return pl.pallas_call(
        leave,
        out_shape=tuple(like(v) for v in results),
        in_specs=[hbm] * 5,
        out_specs=(hbm,) * 5,
        scratch_shapes=[pltpu.VMEM(v.shape, v.dtype) for v in results] + [dma((2, 5))],
        compiler_params=pltpu.CompilerParams(vmem_limit_bytes=VMEM_BYTES),
        name="leave",
    )(*results)


def solution(mesh):
    Z = mesh.shape["dp"] // Y
    M = mesh.shape["mp"]
    placed = (
        P("dp", "mp"),
        P("dp", "mp"),
        P("dp", None, None, "mp"),
        P(),
        P(),
        P("dp", None),
        P(),
        P(),
        P("dp", "mp"),
    )
    return jax.shard_map(
        functools.partial(local, Z, M),
        mesh=mesh,
        in_specs=placed,
        out_specs=(
            P("dp", "mp"),
            P("dp", "mp"),
            P("dp", "mp"),
            P("dp", "mp"),
            P("dp", None, None, "mp"),
        ),
        check_vma=False,
    )
```

```python
import functools

import jax
import jax.numpy as jnp
from jax import lax
from jax.experimental import pallas as pl
from jax.experimental.pallas import tpu as pltpu
from jax.sharding import PartitionSpec as P

HEAD_DIM = 128
IT = 32
IMG_DEV = 2
TOK = 128
Y = 8
G = 4
EPS = 1e-05
VMEM_BYTES = 63 * 1024 * 1024
MESH = pl.DeviceIdType.MESH
F32 = jnp.float32
BF16 = jnp.bfloat16
NT = (((1,), (1,)), ((), ()))
TN = (((0,), (0,)), ((), ()))
NN = (((1,), (0,)), ((), ()))


def dot(left, right, dims):
    return lax.dot_general(left, right, dims, preferred_element_type=F32)


def kernel(
    Z,
    M,
    cites,
    hidden_ref,
    query_ref,
    kv_ref,
    owner_ref,
    citation_ref,
    mask_ref,
    gate_ref,
    gain_ref,
    upstream_ref,
    block_ref,
    normed_ref,
    hgrad_ref,
    qgrad_ref,
    kvgrad_ref,
    owner,
    citation,
    gate_in,
    gains,
    pos_make,
    pos,
    k_all,
    v_all,
    q_all,
    hid_all,
    ups_all,
    mask_all,
    ksel,
    vsel,
    probs,
    plow,
    plow_t,
    block_out,
    normed_out,
    hgrad_out,
    dq_out,
    out_grad,
    stat_out,
    stat_in,
    score_grad,
    dense_k,
    dense_v,
    sums,
    sib_out,
    sib_in,
    rs_out,
    rs_in,
    fin_sib,
    fin_out,
    sent,
    kv_r,
    token_r,
    ag_r,
    sa_r,
    stat_r,
    out_r,
    sr_r,
    rs_r,
    fs_r,
    loc,
):
    T = Z // 2
    X = M // 2
    kv_all = (k_all, v_all)
    n_rows = Z * Y * IMG_DEV
    feats = M * G * HEAD_DIM
    dp = lax.axis_index("dp")
    mp = lax.axis_index("mp")
    z, y = dp // Y, dp % Y
    x, core = mp // 2, mp % 2
    a, b = y // G, y % G
    right = (lax.rem(z + 1, Z) * Y + y, mp)
    left = (lax.rem(z + Z - 1, Z) * Y + y, mp)
    sibling = (dp, x * 2 + 1 - core)
    in_group = a == core

    def peer(i):
        return (z * Y + core * G + i, x * 2 + a)

    far_first = sorted(range(1, X * Y), key=lambda k: -min(k % Y, Y - k % Y) - min(k // Y, X - k // Y))
    head_peers = [
        (z * Y + lax.rem(y + k % Y, Y), lax.rem(x + k // Y, X) * 2 + core) for k in far_first
    ]

    barrier = pltpu.get_barrier_semaphore()
    others = [peer(lax.rem(b + k, G)) for k in range(1, G)] + [right, left, sibling]
    others += head_peers
    for other in others:
        pl.semaphore_signal(barrier, inc=1, device_id=other, device_id_type=MESH)

    @pl.when(jnp.logical_not(in_group))
    def _():
        pl.semaphore_signal(barrier, inc=1, device_id=peer(b), device_id_type=MESH)

    own_copies = []
    for source, place in (
        (citation_ref, citation),
        (owner_ref, owner),
        (gate_ref, gate_in),
        (gain_ref, gains),
    ):
        copy = pltpu.make_async_copy(source, place, loc.at[len(own_copies)])
        copy.start()
        own_copies.append(copy)

    pl.semaphore_wait(barrier, len(others) + jnp.where(in_group, 0, 1))

    def remote(src, dst, ssem, rsem, device):
        return pltpu.make_async_remote_copy(
            src_ref=src,
            dst_ref=dst,
            send_sem=ssem,
            recv_sem=rsem,
            device_id=device,
            device_id_type=MESH,
        )

    GROUP, RING, PAIR, STAT, SUM_RING, SUM_PAIR = range(6)

    def give(i, src, dst, rsem):
        mine = in_group & (i == b)

        @pl.when(mine)
        def _():
            pltpu.make_async_copy(src, dst, rsem).start()

        @pl.when(jnp.logical_not(mine))
        def _():
            remote(src, dst, sent.at[GROUP], rsem, peer(i)).start()

    def landed(buffer, rsem):
        pltpu.make_async_copy(buffer, buffer, rsem).wait()

    def left_here(buffer, kind):
        pltpu.make_async_copy(buffer, buffer, sent.at[kind]).wait()

    def head(i):
        return pl.ds(pl.multiple_of(i * HEAD_DIM, HEAD_DIM), HEAD_DIM)

    def kv_src(kv, i):
        return kv_ref.at[:, kv, :, head(i)]

    def piece(kv, zb, yy):
        return kv_all[kv].at[pl.ds((zb * Y + yy) * IMG_DEV, IMG_DEV)]

    turn = [lax.rem(b + k, G) for k in range(G)]
    for kv in (0, 1):
        for i in turn:
            give(i, kv_src(kv, i), piece(kv, z, y), kv_r.at[kv, b // 2])

    onward = (jnp.where(core == 0, right[0], left[0]), mp)
    block_rows = Y * IMG_DEV
    sub_rows = block_rows // 4
    mine = [2 * core, 2 * core + 1]
    theirs = [2 - 2 * core, 3 - 2 * core]

    def sub_block(kv, zb, h):
        return kv_all[kv].at[pl.ds(zb * block_rows + h * sub_rows, sub_rows)]

    def ring_copy(kv, t, zb, h):
        block = sub_block(kv, zb, h)
        return remote(block, block, sent.at[RING], ag_r.at[kv, t, h], onward)

    def share(kv, zb, which):
        return kv_all[kv].at[pl.ds((zb * Y + which * G) * IMG_DEV, G * IMG_DEV)]

    def to_sibling(block, rsem):
        remote(block, block, sent.at[PAIR], rsem, sibling).start()

    def from_sibling(kv):
        landed(kv_all[kv].at[pl.ds(0, (Z - 1) * G * IMG_DEV)], sa_r.at[1, kv])

    for kv in (0, 1):
        for h in (0, 1):
            landed(sub_block(kv, z, mine[h]), kv_r.at[kv, h])
            ring_copy(kv, 0, z, mine[h]).start()
        to_sibling(share(kv, z, core), sa_r.at[0, kv])
    for kv in (0, 1):
        landed(share(kv, z, 1 - core), sa_r.at[0, kv])
        for h in theirs:
            ring_copy(kv, 0, z, h).start()

    token_inputs = (query_ref, q_all), (hidden_ref, hid_all), (upstream_ref, ups_all)
    for i in turn:
        give(i, mask_ref, mask_all.at[b], token_r.at[0])
    for n, (source, place) in enumerate(token_inputs):
        for i in turn:
            give(i, source.at[:, head(i)], place.at[b], token_r.at[min(n, 1)])

    for copy in own_copies:
        copy.wait()
    first = z * Y + core * G

    def row_of(s, n):
        return owner[citation[n, first + s]]

    lanes = lax.broadcasted_iota(jnp.int32, (8, n_rows), 1)
    sublanes = lax.broadcasted_iota(jnp.int32, (8, n_rows), 0)

    def find(n, found):
        for s in range(G):
            found = jnp.where((sublanes == s) & (lanes == row_of(s, n)), n, found)
        return found

    pos_make[...] = lax.fori_loop(0, cites, find, jnp.full((8, n_rows), cites, jnp.int32))
    pos_copy = pltpu.make_async_copy(pos_make, pos, loc.at[4])
    pos_copy.start()

    def ring_step(kv, t):
        zb = lax.rem(z + jnp.where(core == 0, Z - t, t), Z)
        for n, h in enumerate(mine + theirs if t < T else mine):
            ring_copy(kv, t - 1, zb, h).wait_recv()
            if t < T - 1 or (t == T - 1 and n < 2):
                ring_copy(kv, t, zb, h).start()
        if t < T:
            to_sibling(kv_all[kv].at[pl.ds(zb * block_rows, block_rows)], sa_r.at[1, kv])
        else:
            to_sibling(share(kv, zb, core), sa_r.at[1, kv])

    for t in range(1, T):
        ring_step(0, t)
        ring_step(1, t)
    ring_step(0, T)
    from_sibling(0)
    landed(probs.at[:, pl.ds(0, 96)], token_r.at[0])

    scale = HEAD_DIM**-0.5
    log2e = 1.4426950408889634

    def scores_of(s, _):
        for n in range(cites):
            ksel[s, n * IT : (n + 1) * IT] = k_all[row_of(s, n)]
        scores = dot(ksel[s], q_all[s], NT) * (scale * log2e)
        scores = scores.reshape(cites, IT, TOK)
        scores += jnp.where(mask_all[s] > 0, 0.0, -1e30).astype(F32)[:, None, :]
        top = jnp.max(jnp.max(scores, axis=0), axis=0, keepdims=True)
        weights = jnp.exp2(scores - top[None])
        total = jnp.sum(jnp.sum(weights, axis=0), axis=0, keepdims=True)
        weights = (weights * (1.0 / total)[None]).reshape(cites * IT, TOK)
        probs[s] = weights
        rounded = weights.astype(BF16)
        plow[s, :cites] = rounded.reshape(cites, IT, TOK)
        plow[s, cites] = jnp.zeros((IT, TOK), BF16)
        plow_t[s] = rounded.T
        return 0

    lax.fori_loop(0, G, scores_of, 0, unroll=True)

    ring_step(1, T)
    from_sibling(1)
    landed(probs.at[:, pl.ds(0, 128)], token_r.at[1])

    gate = jnp.tanh(jnp.full((1, HEAD_DIM), gate_in[0], F32))
    gain = gains[pl.ds(x * Y + y, 1), :]
    stat_lane = lax.broadcasted_iota(jnp.int32, (TOK, HEAD_DIM), 1)

    def attend(s, stats):
        for n in range(cites):
            vsel[s, n * IT : (n + 1) * IT] = v_all[row_of(s, n)]
        attended = dot(plow_t[s], vsel[s], NN)
        block = (hid_all[s].astype(F32) + gate * attended).astype(BF16)
        block_out[s] = block
        wide = block.astype(F32)
        square = jnp.sum(wide * wide, axis=1, keepdims=True)
        inner = jnp.sum(gain * ups_all[s].astype(F32) * wide, axis=1, keepdims=True)
        stats = jnp.where(stat_lane == 2 * s, square, stats)
        return jnp.where(stat_lane == 2 * s + 1, inner, stats)

    stats = lax.fori_loop(0, G, attend, jnp.zeros((TOK, HEAD_DIM), F32), unroll=True)

    stat_out[...] = jnp.transpose(stats)[:8]
    slot = x * Y + y
    stat_in[slot] = stat_out[...]
    for other in head_peers:
        remote(stat_out, stat_in.at[slot], sent.at[STAT], stat_r.at[0], other).start()
    for s in range(G):
        give(s, block_out.at[s], block_ref.at[:, head(b)], out_r.at[0])

    def target(which, n):
        to_right = (core == 0) if which else (core == 1)
        return lax.rem(z + jnp.where(to_right, T - n, Z - T + n), Z)

    def spread(dense, source, which, n):
        base = target(which, n) * block_rows
        if n == 0:
            base += (core if which else 1 - core) * (block_rows // 2)
        for r in range(block_rows if n else block_rows // 2):
            for s in range(G):
                block = source[s, pos[s, base + r]]
                dense[which, n, r * IT : (r + 1) * IT, s * TOK : (s + 1) * TOK] = block

    pos_copy.wait()
    for n in range(T + 1):
        for which in (0, 1) if n < T else (1,):
            spread(dense_v, plow, which, n)
    landed(stat_in.at[pl.ds(0, X * Y - 1)], stat_r.at[0])
    total = jnp.sum(stat_in[...], axis=0)
    columns = jnp.transpose(jnp.concatenate([total] * (TOK // 8), axis=0))

    for s in range(G):
        inverse = lax.rsqrt(columns[:, 2 * s : 2 * s + 1] / feats + EPS)
        slope = inverse * inverse * inverse * columns[:, 2 * s + 1 : 2 * s + 2] / feats
        wide = block_out[s].astype(F32)
        grad = inverse * (gain * ups_all[s].astype(F32)) - wide * slope
        out_grad[s] = (gate * grad).astype(BF16)
        hgrad_out[s] = grad.astype(BF16)
        normed_out[s] = (wide * inverse * gain).astype(BF16)

    def dense_sum(kv, which, n):
        tokens = (q_all, out_grad)[kv][...].reshape(G * TOK, HEAD_DIM)
        rows = block_rows if n else block_rows // 2
        left_side = (dense_k, dense_v)[kv][which, n, : rows * IT]
        return dot(left_side, tokens, NN).reshape(rows, IT, HEAD_DIM)

    def for_sibling(kv):
        for n in range(T):
            if kv == 0:
                spread(dense_k, score_grad, 0, n)
            rows = pl.ds(0, block_rows if n else block_rows // 2)
            sib_out[kv, n, rows] = dense_sum(kv, 0, n).astype(BF16)
            remote(
                sib_out.at[kv, n, rows],
                sib_in.at[kv, n, rows],
                sent.at[SUM_PAIR],
                sr_r.at[kv, min(n, 1)],
                sibling,
            ).start()

    def pass_on(kv, t, h):
        return remote(
            rs_out.at[kv, t, h],
            rs_in.at[kv, t, h],
            sent.at[SUM_RING],
            rs_r.at[kv, t, h],
            onward,
        )

    def sum_start(kv):
        if kv == 0:
            spread(dense_k, score_grad, 1, 0)
        value = dense_sum(kv, 1, 0)
        landed(sib_in.at[kv, 0, pl.ds(0, block_rows // 2)], sr_r.at[kv, 0])
        value = (value + sib_in[kv, 0, : block_rows // 2].astype(F32)).astype(BF16)
        for h in (0, 1):
            rs_out[kv, 0, h] = value[h * sub_rows : (h + 1) * sub_rows]
            pass_on(kv, 0, h).start()

    def sum_own(kv):
        landed(sib_in.at[kv, pl.ds(1, T - 1)], sr_r.at[kv, 1])
        for n in range(1, T + 1):
            if kv == 0:
                spread(dense_k, score_grad, 1, n)
            value = dense_sum(kv, 1, n)
            sums[kv, n - 1] = value + sib_in[kv, n].astype(F32) if n < T else value

    def with_arrived(kv, t, h, slot):
        pass_on(kv, t - 1, slot).wait_recv()
        return sums[kv, t - 1, pl.ds(h * sub_rows, sub_rows)] + rs_in[kv, t - 1, slot].astype(F32)

    def sum_step(kv, t):
        for n, h in enumerate(theirs + mine):
            if t == 1 and n < 2:
                value = sums[kv, 0, pl.ds(h * sub_rows, sub_rows)]
            else:
                value = with_arrived(kv, t, h, n - 2 if t == 1 else h)
            rs_out[kv, t, h] = value.astype(BF16)
            pass_on(kv, t, h).start()

    def last_exchange(kv):
        return remote(fin_sib.at[0, kv], fin_sib.at[1, kv], sent.at[SUM_PAIR], fs_r.at[kv], sibling)

    def sum_end_theirs(kv):
        for n, h in enumerate(theirs):
            value = with_arrived(kv, T, h, h).astype(BF16)
            fin_sib[0, kv, n * sub_rows : (n + 1) * sub_rows] = value
        last_exchange(kv).start()

    def sum_end(kv):
        values = [with_arrived(kv, T, h, h) for h in mine]
        last_exchange(kv).wait_recv()
        for n, value in enumerate(values):
            rows = slice(n * sub_rows, (n + 1) * sub_rows)
            fin_out[kv, rows] = (value + fin_sib[1, kv, rows].astype(F32)).astype(BF16)
        for i in range(G):
            piece_out = fin_out.at[kv, pl.ds(i * IMG_DEV, IMG_DEV)]
            give(i, piece_out, kvgrad_ref.at[:, kv, :, head(b)], out_r.at[0])

    for_sibling(1)

    def backward(s, _):
        weights = probs[s]
        prob_grad = dot(vsel[s], out_grad[s], NT)
        mean = jnp.sum(weights * prob_grad, axis=0, keepdims=True)
        grad = (weights * (prob_grad - mean) * scale).astype(BF16)
        score_grad[s, :cites] = grad.reshape(cites, IT, TOK)
        score_grad[s, cites] = jnp.zeros((IT, TOK), BF16)
        return 0

    lax.fori_loop(0, G, backward, 0, unroll=True)
    sum_start(1)

    for_sibling(0)
    sum_start(0)
    sum_own(1)
    for s in range(G):
        give(s, hgrad_out.at[s], hgrad_ref.at[:, head(b)], out_r.at[0])
        give(s, normed_out.at[s], normed_ref.at[:, head(b)], out_r.at[0])
    sum_step(1, 1)
    sum_own(0)
    sum_step(0, 1)
    for s in range(G):
        grad = score_grad[s, :cites].reshape(cites * IT, TOK)
        dq_out[s] = dot(grad, ksel[s], TN).astype(BF16)
        give(s, dq_out.at[s], qgrad_ref.at[:, head(b)], out_r.at[0])
    for t in range(2, T):
        sum_step(1, t)
        sum_step(0, t)
    sum_end_theirs(1)
    sum_end_theirs(0)
    sum_end(1)
    sum_end(0)

    left_here(k_all.at[pl.ds(0, (Z - 1) * block_rows)], RING)
    left_here(k_all, PAIR)
    left_here(stat_in.at[pl.ds(0, X * Y - 1)], STAT)
    left_here(k_all.at[pl.ds(0, (Z - 1) * block_rows)], SUM_RING)
    left_here(k_all, SUM_PAIR)
    group_rows = 304 * 2

    @pl.when(in_group)
    def _():
        left_here(probs.at[pl.ds(0, G - 1), pl.ds(0, group_rows)], GROUP)

    @pl.when(jnp.logical_not(in_group))
    def _():
        left_here(probs.at[:, pl.ds(0, group_rows)], GROUP)

    landed(probs.at[:, pl.ds(0, 160 * 2)], out_r.at[0])


def leave(*refs):
    sources, places, stages, sems = refs[:5], refs[5:10], refs[10:15], refs[15]
    loads = [
        pltpu.make_async_copy(s, p, sems.at[0, n]) for n, (s, p) in enumerate(zip(sources, stages))
    ]
    stores = [
        pltpu.make_async_copy(s, p, sems.at[1, n]) for n, (s, p) in enumerate(zip(stages, places))
    ]
    for copy in loads:
        copy.start()
    for load, store in zip(loads, stores):
        load.wait()
        store.start()
    for copy in stores:
        copy.wait()


def local(
    Z,
    M,
    hidden_in,
    queries,
    image_kv,
    image_owner,
    citations,
    cite_mask,
    gate_scalars,
    norm_gain,
    upstream,
):
    cites = cite_mask.shape[1]
    n_rows = Z * Y * IMG_DEV
    T = Z // 2
    hbm = pl.BlockSpec(memory_space=pltpu.HBM)
    heads = (G, TOK, HEAD_DIM)
    share = (G * IMG_DEV, IT, HEAD_DIM)
    block = (Y * IMG_DEV, IT, HEAD_DIM)
    quarter = (Y * IMG_DEV // 4, IT, HEAD_DIM)
    keys = cites * IT
    dma = pltpu.SemaphoreType.DMA
    like = lambda v: jax.ShapeDtypeStruct(v.shape, v.dtype)
    results = pl.pallas_call(
        functools.partial(kernel, Z, M, cites),
        out_shape=(like(hidden_in),) * 4 + (like(image_kv),),
        in_specs=[hbm] * 9,
        out_specs=(hbm,) * 5,
        scratch_shapes=[
            pltpu.SMEM((n_rows,), jnp.int32),
            pltpu.SMEM(citations.shape[::-1], jnp.int32),
            pltpu.SMEM((1,), F32),
            pltpu.VMEM((M * G, HEAD_DIM), F32),
            pltpu.VMEM((8, n_rows), jnp.int32),
            pltpu.SMEM((8, n_rows), jnp.int32),
            pltpu.VMEM((n_rows, IT, HEAD_DIM), BF16),
            pltpu.VMEM((n_rows, IT, HEAD_DIM), BF16),
            pltpu.VMEM(heads, BF16),
            pltpu.VMEM(heads, BF16),
            pltpu.VMEM(heads, BF16),
            pltpu.VMEM((G, cites, TOK), jnp.int32),
            pltpu.VMEM((G, keys, HEAD_DIM), BF16),
            pltpu.VMEM((G, keys, HEAD_DIM), BF16),
            pltpu.VMEM((G, keys, TOK), F32),
            pltpu.VMEM((G, cites + 1, IT, TOK), BF16),
            pltpu.VMEM((G, TOK, keys), BF16),
            pltpu.VMEM(heads, BF16),
            pltpu.VMEM(heads, BF16),
            pltpu.VMEM(heads, BF16),
            pltpu.VMEM(heads, BF16),
            pltpu.VMEM(heads, BF16),
            pltpu.VMEM((8, TOK), F32),
            pltpu.VMEM((M // 2 * Y, 8, TOK), F32),
            pltpu.VMEM((G, cites + 1, IT, TOK), BF16),
            pltpu.VMEM((2, T + 1, Y * IMG_DEV * IT, G * TOK), BF16),
            pltpu.VMEM((2, T + 1, Y * IMG_DEV * IT, G * TOK), BF16),
            pltpu.VMEM((2, T) + block, F32),
            pltpu.VMEM((2, T) + block, BF16),
            pltpu.VMEM((2, T) + block, BF16),
            pltpu.VMEM((2, T, 4) + quarter, BF16),
            pltpu.VMEM((2, T, 4) + quarter, BF16),
            pltpu.VMEM((2, 2) + share, BF16),
            pltpu.VMEM((2,) + share, BF16),
            dma((6,)),
            dma((2, 2)),
            dma((2,)),
            dma((2, T, 4)),
            dma((2, 2)),
            dma((1,)),
            dma((1,)),
            dma((2, 2)),
            dma((2, T, 4)),
            dma((2,)),
            dma((5,)),
        ],
        compiler_params=pltpu.CompilerParams(
            collective_id=0, has_side_effects=True, vmem_limit_bytes=VMEM_BYTES
        ),
        name="attend",
    )(
        hidden_in,
        queries,
        image_kv,
        image_owner,
        citations.T,
        cite_mask.T,
        gate_scalars,
        norm_gain.reshape(M * G, HEAD_DIM),
        upstream,
    )
    return pl.pallas_call(
        leave,
        out_shape=tuple(like(v) for v in results),
        in_specs=[hbm] * 5,
        out_specs=(hbm,) * 5,
        scratch_shapes=[pltpu.VMEM(v.shape, v.dtype) for v in results] + [dma((2, 5))],
        compiler_params=pltpu.CompilerParams(vmem_limit_bytes=VMEM_BYTES),
        name="leave",
    )(*results)


def solution(mesh):
    Z = mesh.shape["dp"] // Y
    M = mesh.shape["mp"]
    placed = (
        P("dp", "mp"),
        P("dp", "mp"),
        P("dp", None, None, "mp"),
        P(),
        P(),
        P("dp", None),
        P(),
        P(),
        P("dp", "mp"),
    )
    return jax.shard_map(
        functools.partial(local, Z, M),
        mesh=mesh,
        in_specs=placed,
        out_specs=(
            P("dp", "mp"),
            P("dp", "mp"),
            P("dp", "mp"),
            P("dp", "mp"),
            P("dp", None, None, "mp"),
        ),
        check_vma=False,
    )
```

```python
import functools

import jax
import jax.numpy as jnp
from jax import lax
from jax.experimental import pallas as pl
from jax.experimental.pallas import tpu as pltpu
from jax.sharding import PartitionSpec as P

HEAD_DIM = 128
IT = 32
IMG_DEV = 2
TOK = 128
Y = 8
G = 4
EPS = 1e-05
VMEM_BYTES = 63 * 1024 * 1024
MESH = pl.DeviceIdType.MESH
F32 = jnp.float32
BF16 = jnp.bfloat16
NT = (((1,), (1,)), ((), ()))
TN = (((0,), (0,)), ((), ()))
NN = (((1,), (0,)), ((), ()))


def dot(left, right, dims):
    return lax.dot_general(left, right, dims, preferred_element_type=F32)


def kernel(
    Z,
    M,
    cites,
    hidden_ref,
    query_ref,
    kv_ref,
    owner_ref,
    citation_ref,
    mask_ref,
    gate_ref,
    gain_ref,
    upstream_ref,
    block_ref,
    normed_ref,
    hgrad_ref,
    qgrad_ref,
    kvgrad_ref,
    owner,
    citation,
    gate_in,
    gains,
    pos_make,
    pos,
    k_all,
    v_all,
    q_all,
    hid_all,
    ups_all,
    mask_all,
    ksel,
    vsel,
    probs,
    plow,
    plow_t,
    block_out,
    normed_out,
    hgrad_out,
    dq_out,
    out_grad,
    stat_out,
    stat_in,
    score_grad,
    dense_k,
    dense_v,
    sums,
    sib_out,
    sib_in,
    rs_out,
    rs_in,
    fin_sib,
    fin_out,
    sent,
    kv_r,
    token_r,
    ag_r,
    sa_r,
    stat_r,
    out_r,
    sr_r,
    rs_r,
    fs_r,
    loc,
):
    T = Z // 2
    X = M // 2
    kv_all = (k_all, v_all)
    n_rows = Z * Y * IMG_DEV
    feats = M * G * HEAD_DIM
    dp = lax.axis_index("dp")
    mp = lax.axis_index("mp")
    z, y = dp // Y, dp % Y
    x, core = mp // 2, mp % 2
    a, b = y // G, y % G
    right = (lax.rem(z + 1, Z) * Y + y, mp)
    left = (lax.rem(z + Z - 1, Z) * Y + y, mp)
    sibling = (dp, x * 2 + 1 - core)
    in_group = a == core

    def peer(i):
        return (z * Y + core * G + i, x * 2 + a)

    far_first = sorted(range(1, X * Y), key=lambda k: -min(k % Y, Y - k % Y) - min(k // Y, X - k // Y))
    head_peers = [
        (z * Y + lax.rem(y + k % Y, Y), lax.rem(x + k // Y, X) * 2 + core) for k in far_first
    ]

    barrier = pltpu.get_barrier_semaphore()
    others = [peer(lax.rem(b + k, G)) for k in range(1, G)] + [right, left, sibling]
    others += head_peers
    for other in others:
        pl.semaphore_signal(barrier, inc=1, device_id=other, device_id_type=MESH)

    @pl.when(jnp.logical_not(in_group))
    def _():
        pl.semaphore_signal(barrier, inc=1, device_id=peer(b), device_id_type=MESH)

    own_copies = []
    for source, place in (
        (citation_ref, citation),
        (owner_ref, owner),
        (gate_ref, gate_in),
        (gain_ref, gains),
    ):
        copy = pltpu.make_async_copy(source, place, loc.at[len(own_copies)])
        copy.start()
        own_copies.append(copy)

    pl.semaphore_wait(barrier, len(others) + jnp.where(in_group, 0, 1))

    def remote(src, dst, ssem, rsem, device):
        return pltpu.make_async_remote_copy(
            src_ref=src,
            dst_ref=dst,
            send_sem=ssem,
            recv_sem=rsem,
            device_id=device,
            device_id_type=MESH,
        )

    GROUP, RING, PAIR, STAT, SUM_RING, SUM_PAIR = range(6)

    def give(i, src, dst, rsem):
        mine = in_group & (i == b)

        @pl.when(mine)
        def _():
            pltpu.make_async_copy(src, dst, rsem).start()

        @pl.when(jnp.logical_not(mine))
        def _():
            remote(src, dst, sent.at[GROUP], rsem, peer(i)).start()

    def landed(buffer, rsem):
        pltpu.make_async_copy(buffer, buffer, rsem).wait()

    def left_here(buffer, kind):
        pltpu.make_async_copy(buffer, buffer, sent.at[kind]).wait()

    def head(i):
        return pl.ds(pl.multiple_of(i * HEAD_DIM, HEAD_DIM), HEAD_DIM)

    def kv_src(kv, i):
        return kv_ref.at[:, kv, :, head(i)]

    def piece(kv, zb, yy):
        return kv_all[kv].at[pl.ds((zb * Y + yy) * IMG_DEV, IMG_DEV)]

    turn = [lax.rem(b + k, G) for k in range(G)]
    for kv in (0, 1):
        for i in turn:
            give(i, kv_src(kv, i), piece(kv, z, y), kv_r.at[kv, b // 2])

    onward = (jnp.where(core == 0, right[0], left[0]), mp)
    block_rows = Y * IMG_DEV
    sub_rows = block_rows // 4
    mine = [2 * core, 2 * core + 1]
    theirs = [2 - 2 * core, 3 - 2 * core]

    def sub_block(kv, zb, h):
        return kv_all[kv].at[pl.ds(zb * block_rows + h * sub_rows, sub_rows)]

    def ring_copy(kv, t, zb, h):
        block = sub_block(kv, zb, h)
        return remote(block, block, sent.at[RING], ag_r.at[kv, t, h], onward)

    def share(kv, zb, which):
        return kv_all[kv].at[pl.ds((zb * Y + which * G) * IMG_DEV, G * IMG_DEV)]

    def to_sibling(block, rsem):
        remote(block, block, sent.at[PAIR], rsem, sibling).start()

    def from_sibling(kv):
        landed(kv_all[kv].at[pl.ds(0, (Z - 1) * G * IMG_DEV)], sa_r.at[1, kv])

    for kv in (0, 1):
        for h in (0, 1):
            landed(sub_block(kv, z, mine[h]), kv_r.at[kv, h])
            ring_copy(kv, 0, z, mine[h]).start()
        to_sibling(share(kv, z, core), sa_r.at[0, kv])
    for kv in (0, 1):
        landed(share(kv, z, 1 - core), sa_r.at[0, kv])
        for h in theirs:
            ring_copy(kv, 0, z, h).start()

    token_inputs = (query_ref, q_all), (hidden_ref, hid_all), (upstream_ref, ups_all)
    for i in turn:
        give(i, mask_ref, mask_all.at[b], token_r.at[0])
    for n, (source, place) in enumerate(token_inputs):
        for i in turn:
            give(i, source.at[:, head(i)], place.at[b], token_r.at[min(n, 1)])

    for copy in own_copies:
        copy.wait()
    first = z * Y + core * G

    def row_of(s, n):
        return owner[citation[n, first + s]]

    lanes = lax.broadcasted_iota(jnp.int32, (8, n_rows), 1)
    sublanes = lax.broadcasted_iota(jnp.int32, (8, n_rows), 0)

    def find(n, found):
        for s in range(G):
            found = jnp.where((sublanes == s) & (lanes == row_of(s, n)), n, found)
        return found

    pos_make[...] = lax.fori_loop(0, cites, find, jnp.full((8, n_rows), cites, jnp.int32))
    pos_copy = pltpu.make_async_copy(pos_make, pos, loc.at[4])
    pos_copy.start()

    def ring_step(kv, t):
        zb = lax.rem(z + jnp.where(core == 0, Z - t, t), Z)
        for n, h in enumerate(mine + theirs if t < T else mine):
            ring_copy(kv, t - 1, zb, h).wait_recv()
            if t < T - 1 or (t == T - 1 and n < 2):
                ring_copy(kv, t, zb, h).start()
        if t < T:
            to_sibling(kv_all[kv].at[pl.ds(zb * block_rows, block_rows)], sa_r.at[1, kv])
        else:
            to_sibling(share(kv, zb, core), sa_r.at[1, kv])

    for t in range(1, T):
        ring_step(0, t)
        ring_step(1, t)
    ring_step(0, T)
    from_sibling(0)
    landed(probs.at[:, pl.ds(0, 96)], token_r.at[0])

    scale = HEAD_DIM**-0.5
    log2e = 1.4426950408889634

    def scores_of(s, _):
        for n in range(cites):
            ksel[s, n * IT : (n + 1) * IT] = k_all[row_of(s, n)]
        scores = dot(ksel[s], q_all[s], NT) * (scale * log2e)
        scores = scores.reshape(cites, IT, TOK)
        scores += jnp.where(mask_all[s] > 0, 0.0, -1e30).astype(F32)[:, None, :]
        top = jnp.max(jnp.max(scores, axis=0), axis=0, keepdims=True)
        weights = jnp.exp2(scores - top[None])
        total = jnp.sum(jnp.sum(weights, axis=0), axis=0, keepdims=True)
        weights = (weights * (1.0 / total)[None]).reshape(cites * IT, TOK)
        probs[s] = weights
        rounded = weights.astype(BF16)
        plow[s, :cites] = rounded.reshape(cites, IT, TOK)
        plow[s, cites] = jnp.zeros((IT, TOK), BF16)
        plow_t[s] = rounded.T
        return 0

    ring_step(1, T)
    lax.fori_loop(0, G, scores_of, 0, unroll=True)

    from_sibling(1)
    landed(probs.at[:, pl.ds(0, 128)], token_r.at[1])

    gate = jnp.tanh(jnp.full((1, HEAD_DIM), gate_in[0], F32))
    gain = gains[pl.ds(x * Y + y, 1), :]
    stat_lane = lax.broadcasted_iota(jnp.int32, (TOK, HEAD_DIM), 1)

    def attend(s, stats):
        for n in range(cites):
            vsel[s, n * IT : (n + 1) * IT] = v_all[row_of(s, n)]
        attended = dot(plow_t[s], vsel[s], NN)
        block = (hid_all[s].astype(F32) + gate * attended).astype(BF16)
        block_out[s] = block
        wide = block.astype(F32)
        square = jnp.sum(wide * wide, axis=1, keepdims=True)
        inner = jnp.sum(gain * ups_all[s].astype(F32) * wide, axis=1, keepdims=True)
        stats = jnp.where(stat_lane == 2 * s, square, stats)
        return jnp.where(stat_lane == 2 * s + 1, inner, stats)

    stats = lax.fori_loop(0, G, attend, jnp.zeros((TOK, HEAD_DIM), F32), unroll=True)

    stat_out[...] = jnp.transpose(stats)[:8]
    slot = x * Y + y
    stat_in[slot] = stat_out[...]
    for other in head_peers:
        remote(stat_out, stat_in.at[slot], sent.at[STAT], stat_r.at[0], other).start()
    for s in range(G):
        give(s, block_out.at[s], block_ref.at[:, head(b)], out_r.at[0])

    def target(which, n):
        to_right = (core == 0) if which else (core == 1)
        return lax.rem(z + jnp.where(to_right, T - n, Z - T + n), Z)

    def spread(dense, source, which, n):
        base = target(which, n) * block_rows
        if n == 0:
            base += (core if which else 1 - core) * (block_rows // 2)
        for r in range(block_rows if n else block_rows // 2):
            for s in range(G):
                block = source[s, pos[s, base + r]]
                dense[which, n, r * IT : (r + 1) * IT, s * TOK : (s + 1) * TOK] = block

    pos_copy.wait()
    for n in range(T + 1):
        for which in (0, 1) if n < T else (1,):
            spread(dense_v, plow, which, n)
    landed(stat_in.at[pl.ds(0, X * Y - 1)], stat_r.at[0])
    total = jnp.sum(stat_in[...], axis=0)
    columns = jnp.transpose(jnp.concatenate([total] * (TOK // 8), axis=0))

    for s in range(G):
        inverse = lax.rsqrt(columns[:, 2 * s : 2 * s + 1] / feats + EPS)
        slope = inverse * inverse * inverse * columns[:, 2 * s + 1 : 2 * s + 2] / feats
        wide = block_out[s].astype(F32)
        grad = inverse * (gain * ups_all[s].astype(F32)) - wide * slope
        out_grad[s] = (gate * grad).astype(BF16)
        hgrad_out[s] = grad.astype(BF16)
        normed_out[s] = (wide * inverse * gain).astype(BF16)

    def dense_sum(kv, which, n):
        tokens = (q_all, out_grad)[kv][...].reshape(G * TOK, HEAD_DIM)
        rows = block_rows if n else block_rows // 2
        left_side = (dense_k, dense_v)[kv][which, n, : rows * IT]
        return dot(left_side, tokens, NN).reshape(rows, IT, HEAD_DIM)

    def for_sibling(kv):
        for n in range(T):
            if kv == 0:
                spread(dense_k, score_grad, 0, n)
            rows = pl.ds(0, block_rows if n else block_rows // 2)
            sib_out[kv, n, rows] = dense_sum(kv, 0, n).astype(BF16)
            remote(
                sib_out.at[kv, n, rows],
                sib_in.at[kv, n, rows],
                sent.at[SUM_PAIR],
                sr_r.at[kv, min(n, 1)],
                sibling,
            ).start()

    def pass_on(kv, t, h):
        return remote(
            rs_out.at[kv, t, h],
            rs_in.at[kv, t, h],
            sent.at[SUM_RING],
            rs_r.at[kv, t, h],
            onward,
        )

    def sum_start(kv):
        if kv == 0:
            spread(dense_k, score_grad, 1, 0)
        value = dense_sum(kv, 1, 0)
        landed(sib_in.at[kv, 0, pl.ds(0, block_rows // 2)], sr_r.at[kv, 0])
        value = (value + sib_in[kv, 0, : block_rows // 2].astype(F32)).astype(BF16)
        for h in (0, 1):
            rs_out[kv, 0, h] = value[h * sub_rows : (h + 1) * sub_rows]
            pass_on(kv, 0, h).start()

    def sum_own(kv):
        landed(sib_in.at[kv, pl.ds(1, T - 1)], sr_r.at[kv, 1])
        for n in range(1, T + 1):
            if kv == 0:
                spread(dense_k, score_grad, 1, n)
            value = dense_sum(kv, 1, n)
            sums[kv, n - 1] = value + sib_in[kv, n].astype(F32) if n < T else value

    def with_arrived(kv, t, h, slot):
        pass_on(kv, t - 1, slot).wait_recv()
        return sums[kv, t - 1, pl.ds(h * sub_rows, sub_rows)] + rs_in[kv, t - 1, slot].astype(F32)

    def sum_step(kv, t):
        for n, h in enumerate(theirs + mine):
            if t == 1 and n < 2:
                value = sums[kv, 0, pl.ds(h * sub_rows, sub_rows)]
            else:
                value = with_arrived(kv, t, h, n - 2 if t == 1 else h)
            rs_out[kv, t, h] = value.astype(BF16)
            pass_on(kv, t, h).start()

    def last_exchange(kv):
        return remote(fin_sib.at[0, kv], fin_sib.at[1, kv], sent.at[SUM_PAIR], fs_r.at[kv], sibling)

    def sum_end_theirs(kv):
        for n, h in enumerate(theirs):
            value = with_arrived(kv, T, h, h).astype(BF16)
            fin_sib[0, kv, n * sub_rows : (n + 1) * sub_rows] = value
        last_exchange(kv).start()

    def sum_end(kv):
        values = [with_arrived(kv, T, h, h) for h in mine]
        last_exchange(kv).wait_recv()
        for n, value in enumerate(values):
            rows = slice(n * sub_rows, (n + 1) * sub_rows)
            fin_out[kv, rows] = (value + fin_sib[1, kv, rows].astype(F32)).astype(BF16)
        for i in range(G):
            piece_out = fin_out.at[kv, pl.ds(i * IMG_DEV, IMG_DEV)]
            give(i, piece_out, kvgrad_ref.at[:, kv, :, head(b)], out_r.at[0])

    for_sibling(1)

    def backward(s, _):
        weights = probs[s]
        prob_grad = dot(vsel[s], out_grad[s], NT)
        mean = jnp.sum(weights * prob_grad, axis=0, keepdims=True)
        grad = (weights * (prob_grad - mean) * scale).astype(BF16)
        score_grad[s, :cites] = grad.reshape(cites, IT, TOK)
        score_grad[s, cites] = jnp.zeros((IT, TOK), BF16)
        return 0

    lax.fori_loop(0, G, backward, 0, unroll=True)
    sum_start(1)

    for_sibling(0)
    sum_start(0)
    sum_own(1)
    for s in range(G):
        give(s, hgrad_out.at[s], hgrad_ref.at[:, head(b)], out_r.at[0])
        give(s, normed_out.at[s], normed_ref.at[:, head(b)], out_r.at[0])
    sum_step(1, 1)
    sum_own(0)
    sum_step(0, 1)
    for s in range(G):
        grad = score_grad[s, :cites].reshape(cites * IT, TOK)
        dq_out[s] = dot(grad, ksel[s], TN).astype(BF16)
        give(s, dq_out.at[s], qgrad_ref.at[:, head(b)], out_r.at[0])
    for t in range(2, T):
        sum_step(1, t)
        sum_step(0, t)
    sum_end_theirs(1)
    sum_end_theirs(0)
    sum_end(1)
    sum_end(0)

    left_here(k_all.at[pl.ds(0, (Z - 1) * block_rows)], RING)
    left_here(k_all, PAIR)
    left_here(stat_in.at[pl.ds(0, X * Y - 1)], STAT)
    left_here(k_all.at[pl.ds(0, (Z - 1) * block_rows)], SUM_RING)
    left_here(k_all, SUM_PAIR)
    group_rows = 304 * 2

    @pl.when(in_group)
    def _():
        left_here(probs.at[pl.ds(0, G - 1), pl.ds(0, group_rows)], GROUP)

    @pl.when(jnp.logical_not(in_group))
    def _():
        left_here(probs.at[:, pl.ds(0, group_rows)], GROUP)

    landed(probs.at[:, pl.ds(0, 160 * 2)], out_r.at[0])


def leave(*refs):
    sources, places, stages, sems = refs[:5], refs[5:10], refs[10:15], refs[15]
    loads = [
        pltpu.make_async_copy(s, p, sems.at[0, n]) for n, (s, p) in enumerate(zip(sources, stages))
    ]
    stores = [
        pltpu.make_async_copy(s, p, sems.at[1, n]) for n, (s, p) in enumerate(zip(stages, places))
    ]
    for copy in loads:
        copy.start()
    for load, store in zip(loads, stores):
        load.wait()
        store.start()
    for copy in stores:
        copy.wait()


def local(
    Z,
    M,
    hidden_in,
    queries,
    image_kv,
    image_owner,
    citations,
    cite_mask,
    gate_scalars,
    norm_gain,
    upstream,
):
    cites = cite_mask.shape[1]
    n_rows = Z * Y * IMG_DEV
    T = Z // 2
    hbm = pl.BlockSpec(memory_space=pltpu.HBM)
    heads = (G, TOK, HEAD_DIM)
    share = (G * IMG_DEV, IT, HEAD_DIM)
    block = (Y * IMG_DEV, IT, HEAD_DIM)
    quarter = (Y * IMG_DEV // 4, IT, HEAD_DIM)
    keys = cites * IT
    dma = pltpu.SemaphoreType.DMA
    like = lambda v: jax.ShapeDtypeStruct(v.shape, v.dtype)
    results = pl.pallas_call(
        functools.partial(kernel, Z, M, cites),
        out_shape=(like(hidden_in),) * 4 + (like(image_kv),),
        in_specs=[hbm] * 9,
        out_specs=(hbm,) * 5,
        scratch_shapes=[
            pltpu.SMEM((n_rows,), jnp.int32),
            pltpu.SMEM(citations.shape[::-1], jnp.int32),
            pltpu.SMEM((1,), F32),
            pltpu.VMEM((M * G, HEAD_DIM), F32),
            pltpu.VMEM((8, n_rows), jnp.int32),
            pltpu.SMEM((8, n_rows), jnp.int32),
            pltpu.VMEM((n_rows, IT, HEAD_DIM), BF16),
            pltpu.VMEM((n_rows, IT, HEAD_DIM), BF16),
            pltpu.VMEM(heads, BF16),
            pltpu.VMEM(heads, BF16),
            pltpu.VMEM(heads, BF16),
            pltpu.VMEM((G, cites, TOK), jnp.int32),
            pltpu.VMEM((G, keys, HEAD_DIM), BF16),
            pltpu.VMEM((G, keys, HEAD_DIM), BF16),
            pltpu.VMEM((G, keys, TOK), F32),
            pltpu.VMEM((G, cites + 1, IT, TOK), BF16),
            pltpu.VMEM((G, TOK, keys), BF16),
            pltpu.VMEM(heads, BF16),
            pltpu.VMEM(heads, BF16),
            pltpu.VMEM(heads, BF16),
            pltpu.VMEM(heads, BF16),
            pltpu.VMEM(heads, BF16),
            pltpu.VMEM((8, TOK), F32),
            pltpu.VMEM((M // 2 * Y, 8, TOK), F32),
            pltpu.VMEM((G, cites + 1, IT, TOK), BF16),
            pltpu.VMEM((2, T + 1, Y * IMG_DEV * IT, G * TOK), BF16),
            pltpu.VMEM((2, T + 1, Y * IMG_DEV * IT, G * TOK), BF16),
            pltpu.VMEM((2, T) + block, F32),
            pltpu.VMEM((2, T) + block, BF16),
            pltpu.VMEM((2, T) + block, BF16),
            pltpu.VMEM((2, T, 4) + quarter, BF16),
            pltpu.VMEM((2, T, 4) + quarter, BF16),
            pltpu.VMEM((2, 2) + share, BF16),
            pltpu.VMEM((2,) + share, BF16),
            dma((6,)),
            dma((2, 2)),
            dma((2,)),
            dma((2, T, 4)),
            dma((2, 2)),
            dma((1,)),
            dma((1,)),
            dma((2, 2)),
            dma((2, T, 4)),
            dma((2,)),
            dma((5,)),
        ],
        compiler_params=pltpu.CompilerParams(
            collective_id=0, has_side_effects=True, vmem_limit_bytes=VMEM_BYTES
        ),
        name="attend",
    )(
        hidden_in,
        queries,
        image_kv,
        image_owner,
        citations.T,
        cite_mask.T,
        gate_scalars,
        norm_gain.reshape(M * G, HEAD_DIM),
        upstream,
    )
    return pl.pallas_call(
        leave,
        out_shape=tuple(like(v) for v in results),
        in_specs=[hbm] * 5,
        out_specs=(hbm,) * 5,
        scratch_shapes=[pltpu.VMEM(v.shape, v.dtype) for v in results] + [dma((2, 5))],
        compiler_params=pltpu.CompilerParams(vmem_limit_bytes=VMEM_BYTES),
        name="leave",
    )(*results)


def solution(mesh):
    Z = mesh.shape["dp"] // Y
    M = mesh.shape["mp"]
    placed = (
        P("dp", "mp"),
        P("dp", "mp"),
        P("dp", None, None, "mp"),
        P(),
        P(),
        P("dp", None),
        P(),
        P(),
        P("dp", "mp"),
    )
    return jax.shard_map(
        functools.partial(local, Z, M),
        mesh=mesh,
        in_specs=placed,
        out_specs=(
            P("dp", "mp"),
            P("dp", "mp"),
            P("dp", "mp"),
            P("dp", "mp"),
            P("dp", None, None, "mp"),
        ),
        check_vma=False,
    )
```

```python
import functools

import jax
import jax.numpy as jnp
from jax import lax
from jax.experimental import pallas as pl
from jax.experimental.pallas import tpu as pltpu
from jax.sharding import PartitionSpec as P

HEAD_DIM = 128
IT = 32
IMG_DEV = 2
TOK = 128
Y = 8
G = 4
EPS = 1e-05
VMEM_BYTES = 63 * 1024 * 1024
MESH = pl.DeviceIdType.MESH
F32 = jnp.float32
BF16 = jnp.bfloat16
NT = (((1,), (1,)), ((), ()))
TN = (((0,), (0,)), ((), ()))
NN = (((1,), (0,)), ((), ()))


def dot(left, right, dims):
    return lax.dot_general(left, right, dims, preferred_element_type=F32)


def kernel(
    Z,
    M,
    cites,
    hidden_ref,
    query_ref,
    kv_ref,
    owner_ref,
    citation_ref,
    mask_ref,
    gate_ref,
    gain_ref,
    upstream_ref,
    block_ref,
    normed_ref,
    hgrad_ref,
    qgrad_ref,
    kvgrad_ref,
    owner,
    citation,
    gate_in,
    gains,
    pos_make,
    pos,
    k_all,
    v_all,
    q_all,
    hid_all,
    ups_all,
    mask_all,
    ksel,
    vsel,
    probs,
    plow,
    plow_t,
    block_out,
    normed_out,
    hgrad_out,
    dq_out,
    out_grad,
    stat_out,
    stat_in,
    score_grad,
    dense_k,
    dense_v,
    sums,
    sib_out,
    sib_in,
    rs_out,
    rs_in,
    fin_sib,
    fin_out,
    sent,
    kv_r,
    token_r,
    ag_r,
    sa_r,
    stat_r,
    out_r,
    sr_r,
    rs_r,
    fs_r,
    loc,
):
    T = Z // 2
    X = M // 2
    kv_all = (k_all, v_all)
    n_rows = Z * Y * IMG_DEV
    feats = M * G * HEAD_DIM
    dp = lax.axis_index("dp")
    mp = lax.axis_index("mp")
    z, y = dp // Y, dp % Y
    x, core = mp // 2, mp % 2
    a, b = y // G, y % G
    right = (lax.rem(z + 1, Z) * Y + y, mp)
    left = (lax.rem(z + Z - 1, Z) * Y + y, mp)
    sibling = (dp, x * 2 + 1 - core)
    in_group = a == core

    def peer(i):
        return (z * Y + core * G + i, x * 2 + a)

    far_first = sorted(range(1, X * Y), key=lambda k: -min(k % Y, Y - k % Y) - min(k // Y, X - k // Y))
    head_peers = [
        (z * Y + lax.rem(y + k % Y, Y), lax.rem(x + k // Y, X) * 2 + core) for k in far_first
    ]

    barrier = pltpu.get_barrier_semaphore()
    others = [peer(lax.rem(b + k, G)) for k in range(1, G)] + [right, left, sibling]
    others += head_peers
    for other in others:
        pl.semaphore_signal(barrier, inc=1, device_id=other, device_id_type=MESH)

    @pl.when(jnp.logical_not(in_group))
    def _():
        pl.semaphore_signal(barrier, inc=1, device_id=peer(b), device_id_type=MESH)

    own_copies = []
    for source, place in (
        (citation_ref, citation),
        (owner_ref, owner),
        (gate_ref, gate_in),
        (gain_ref, gains),
    ):
        copy = pltpu.make_async_copy(source, place, loc.at[len(own_copies)])
        copy.start()
        own_copies.append(copy)

    pl.semaphore_wait(barrier, len(others) + jnp.where(in_group, 0, 1))

    def remote(src, dst, ssem, rsem, device):
        return pltpu.make_async_remote_copy(
            src_ref=src,
            dst_ref=dst,
            send_sem=ssem,
            recv_sem=rsem,
            device_id=device,
            device_id_type=MESH,
        )

    GROUP, RING, PAIR, STAT, SUM_RING, SUM_PAIR = range(6)

    def give(i, src, dst, rsem):
        mine = in_group & (i == b)

        @pl.when(mine)
        def _():
            pltpu.make_async_copy(src, dst, rsem).start()

        @pl.when(jnp.logical_not(mine))
        def _():
            remote(src, dst, sent.at[GROUP], rsem, peer(i)).start()

    def landed(buffer, rsem):
        pltpu.make_async_copy(buffer, buffer, rsem).wait()

    def left_here(buffer, kind):
        pltpu.make_async_copy(buffer, buffer, sent.at[kind]).wait()

    def head(i):
        return pl.ds(pl.multiple_of(i * HEAD_DIM, HEAD_DIM), HEAD_DIM)

    def kv_src(kv, i):
        return kv_ref.at[:, kv, :, head(i)]

    def piece(kv, zb, yy):
        return kv_all[kv].at[pl.ds((zb * Y + yy) * IMG_DEV, IMG_DEV)]

    turn = [lax.rem(b + k, G) for k in range(G)]
    for kv in (0, 1):
        for i in turn:
            give(i, kv_src(kv, i), piece(kv, z, y), kv_r.at[kv, b // 2])

    onward = (jnp.where(core == 0, right[0], left[0]), mp)
    block_rows = Y * IMG_DEV
    sub_rows = block_rows // 4
    mine = [2 * core, 2 * core + 1]
    theirs = [2 - 2 * core, 3 - 2 * core]

    def sub_block(kv, zb, h):
        return kv_all[kv].at[pl.ds(zb * block_rows + h * sub_rows, sub_rows)]

    def ring_copy(kv, t, zb, h):
        block = sub_block(kv, zb, h)
        return remote(block, block, sent.at[RING], ag_r.at[kv, t, h], onward)

    def share(kv, zb, which):
        return kv_all[kv].at[pl.ds((zb * Y + which * G) * IMG_DEV, G * IMG_DEV)]

    def to_sibling(block, rsem):
        remote(block, block, sent.at[PAIR], rsem, sibling).start()

    def from_sibling(kv):
        landed(kv_all[kv].at[pl.ds(0, (Z - 1) * G * IMG_DEV)], sa_r.at[1, kv])

    for kv in (0, 1):
        for h in (0, 1):
            landed(sub_block(kv, z, mine[h]), kv_r.at[kv, h])
            ring_copy(kv, 0, z, mine[h]).start()
        to_sibling(share(kv, z, core), sa_r.at[0, kv])
    for kv in (0, 1):
        landed(share(kv, z, 1 - core), sa_r.at[0, kv])
        for h in theirs:
            ring_copy(kv, 0, z, h).start()

    token_inputs = (query_ref, q_all), (hidden_ref, hid_all), (upstream_ref, ups_all)
    for i in turn:
        give(i, mask_ref, mask_all.at[b], token_r.at[0])
    for n, (source, place) in enumerate(token_inputs):
        for i in turn:
            give(i, source.at[:, head(i)], place.at[b], token_r.at[min(n, 1)])

    for copy in own_copies:
        copy.wait()
    first = z * Y + core * G

    def row_of(s, n):
        return owner[citation[n, first + s]]

    lanes = lax.broadcasted_iota(jnp.int32, (8, n_rows), 1)
    sublanes = lax.broadcasted_iota(jnp.int32, (8, n_rows), 0)

    def find(n, found):
        for s in range(G):
            found = jnp.where((sublanes == s) & (lanes == row_of(s, n)), n, found)
        return found

    pos_make[...] = lax.fori_loop(0, cites, find, jnp.full((8, n_rows), cites, jnp.int32))
    pos_copy = pltpu.make_async_copy(pos_make, pos, loc.at[4])
    pos_copy.start()

    def ring_step(kv, t):
        zb = lax.rem(z + jnp.where(core == 0, Z - t, t), Z)
        for n, h in enumerate(mine + theirs if t < T else mine):
            ring_copy(kv, t - 1, zb, h).wait_recv()
            if t < T - 1 or (t == T - 1 and n < 2):
                ring_copy(kv, t, zb, h).start()
        if t < T:
            to_sibling(kv_all[kv].at[pl.ds(zb * block_rows, block_rows)], sa_r.at[1, kv])
        else:
            to_sibling(share(kv, zb, core), sa_r.at[1, kv])

    for t in range(1, T):
        ring_step(0, t)
        ring_step(1, t)
    ring_step(0, T)
    from_sibling(0)
    landed(probs.at[:, pl.ds(0, 96)], token_r.at[0])

    scale = HEAD_DIM**-0.5
    log2e = 1.4426950408889634

    def scores_of(s, _):
        for n in range(cites):
            ksel[s, n * IT : (n + 1) * IT] = k_all[row_of(s, n)]
        scores = dot(ksel[s], q_all[s], NT) * (scale * log2e)
        scores = scores.reshape(cites, IT, TOK)
        scores += jnp.where(mask_all[s] > 0, 0.0, -1e30).astype(F32)[:, None, :]
        top = jnp.max(jnp.max(scores, axis=0), axis=0, keepdims=True)
        weights = jnp.exp2(scores - top[None])
        total = jnp.sum(jnp.sum(weights, axis=0), axis=0, keepdims=True)
        weights = (weights * (1.0 / total)[None]).reshape(cites * IT, TOK)
        probs[s] = weights
        rounded = weights.astype(BF16)
        plow[s, :cites] = rounded.reshape(cites, IT, TOK)
        plow[s, cites] = jnp.zeros((IT, TOK), BF16)
        plow_t[s] = rounded.T
        return 0

    ring_step(1, T)
    lax.fori_loop(0, G, scores_of, 0, unroll=True)

    from_sibling(1)
    landed(probs.at[:, pl.ds(0, 128)], token_r.at[1])

    gate = jnp.tanh(jnp.full((1, HEAD_DIM), gate_in[0], F32))
    gain = gains[pl.ds(x * Y + y, 1), :]
    stat_lane = lax.broadcasted_iota(jnp.int32, (TOK, HEAD_DIM), 1)

    def attend(s, stats):
        for n in range(cites):
            vsel[s, n * IT : (n + 1) * IT] = v_all[row_of(s, n)]
        attended = dot(plow_t[s], vsel[s], NN)
        block = (hid_all[s].astype(F32) + gate * attended).astype(BF16)
        block_out[s] = block
        wide = block.astype(F32)
        square = jnp.sum(wide * wide, axis=1, keepdims=True)
        inner = jnp.sum(gain * ups_all[s].astype(F32) * wide, axis=1, keepdims=True)
        stats = jnp.where(stat_lane == 2 * s, square, stats)
        return jnp.where(stat_lane == 2 * s + 1, inner, stats)

    stats = lax.fori_loop(0, G, attend, jnp.zeros((TOK, HEAD_DIM), F32), unroll=True)

    stat_out[...] = jnp.transpose(stats)[:8]
    slot = x * Y + y
    stat_in[slot] = stat_out[...]
    for other in head_peers:
        remote(stat_out, stat_in.at[slot], sent.at[STAT], stat_r.at[0], other).start()
    for s in range(G):
        give(s, block_out.at[s], block_ref.at[:, head(b)], out_r.at[0])

    def target(which, n):
        to_right = (core == 0) if which else (core == 1)
        return lax.rem(z + jnp.where(to_right, T - n, Z - T + n), Z)

    def spread(dense, source, which, n):
        base = target(which, n) * block_rows
        if n == 0:
            base += (core if which else 1 - core) * (block_rows // 2)
        for r in range(block_rows if n else block_rows // 2):
            for s in range(G):
                block = source[s, pos[s, base + r]]
                dense[which, n, r * IT : (r + 1) * IT, s * TOK : (s + 1) * TOK] = block

    pos_copy.wait()
    for n in range(T + 1):
        for which in (0, 1) if n < T else (1,):
            spread(dense_v, plow, which, n)
    landed(stat_in.at[pl.ds(0, X * Y - 1)], stat_r.at[0])
    total = jnp.sum(stat_in[...], axis=0)
    columns = jnp.transpose(jnp.concatenate([total] * (TOK // 8), axis=0))

    for s in range(G):
        inverse = lax.rsqrt(columns[:, 2 * s : 2 * s + 1] / feats + EPS)
        slope = inverse * inverse * inverse * columns[:, 2 * s + 1 : 2 * s + 2] / feats
        wide = block_out[s].astype(F32)
        grad = inverse * (gain * ups_all[s].astype(F32)) - wide * slope
        out_grad[s] = (gate * grad).astype(BF16)
        hgrad_out[s] = grad.astype(BF16)
        normed_out[s] = (wide * inverse * gain).astype(BF16)

    def dense_sum(kv, which, n):
        tokens = (q_all, out_grad)[kv][...].reshape(G * TOK, HEAD_DIM)
        rows = block_rows if n else block_rows // 2
        left_side = (dense_k, dense_v)[kv][which, n, : rows * IT]
        return dot(left_side, tokens, NN).reshape(rows, IT, HEAD_DIM)

    def for_sibling(kv):
        for n in range(T):
            if kv == 0:
                spread(dense_k, score_grad, 0, n)
            rows = pl.ds(0, block_rows if n else block_rows // 2)
            sib_out[kv, n, rows] = dense_sum(kv, 0, n).astype(BF16)
            remote(
                sib_out.at[kv, n, rows],
                sib_in.at[kv, n, rows],
                sent.at[SUM_PAIR],
                sr_r.at[kv, min(n, 1)],
                sibling,
            ).start()

    def pass_on(kv, t, h):
        return remote(
            rs_out.at[kv, t, h],
            rs_in.at[kv, t, h],
            sent.at[SUM_RING],
            rs_r.at[kv, t, h],
            onward,
        )

    def sum_start(kv):
        if kv == 0:
            spread(dense_k, score_grad, 1, 0)
        value = dense_sum(kv, 1, 0)
        landed(sib_in.at[kv, 0, pl.ds(0, block_rows // 2)], sr_r.at[kv, 0])
        value = (value + sib_in[kv, 0, : block_rows // 2].astype(F32)).astype(BF16)
        for h in (0, 1):
            rs_out[kv, 0, h] = value[h * sub_rows : (h + 1) * sub_rows]
            pass_on(kv, 0, h).start()

    def sum_own(kv):
        landed(sib_in.at[kv, pl.ds(1, T - 1)], sr_r.at[kv, 1])
        for n in range(1, T + 1):
            if kv == 0:
                spread(dense_k, score_grad, 1, n)
            value = dense_sum(kv, 1, n)
            sums[kv, n - 1] = value + sib_in[kv, n].astype(F32) if n < T else value

    def with_arrived(kv, t, h, slot):
        pass_on(kv, t - 1, slot).wait_recv()
        return sums[kv, t - 1, pl.ds(h * sub_rows, sub_rows)] + rs_in[kv, t - 1, slot].astype(F32)

    def sum_step(kv, t):
        for n, h in enumerate(theirs + mine):
            if t == 1 and n < 2:
                value = sums[kv, 0, pl.ds(h * sub_rows, sub_rows)]
            else:
                value = with_arrived(kv, t, h, n - 2 if t == 1 else h)
            rs_out[kv, t, h] = value.astype(BF16)
            pass_on(kv, t, h).start()

    def last_exchange(kv):
        return remote(fin_sib.at[0, kv], fin_sib.at[1, kv], sent.at[SUM_PAIR], fs_r.at[kv], sibling)

    def sum_end_theirs(kv):
        for n, h in enumerate(theirs):
            value = with_arrived(kv, T, h, h).astype(BF16)
            fin_sib[0, kv, n * sub_rows : (n + 1) * sub_rows] = value
        last_exchange(kv).start()

    def sum_end(kv):
        values = [with_arrived(kv, T, h, h) for h in mine]
        last_exchange(kv).wait_recv()
        for n, value in enumerate(values):
            rows = slice(n * sub_rows, (n + 1) * sub_rows)
            fin_out[kv, rows] = (value + fin_sib[1, kv, rows].astype(F32)).astype(BF16)
        for i in range(G):
            piece_out = fin_out.at[kv, pl.ds(i * IMG_DEV, IMG_DEV)]
            give(i, piece_out, kvgrad_ref.at[:, kv, :, head(b)], out_r.at[0])

    for_sibling(1)

    def backward(s, _):
        weights = probs[s]
        prob_grad = dot(vsel[s], out_grad[s], NT)
        mean = jnp.sum(weights * prob_grad, axis=0, keepdims=True)
        grad = (weights * (prob_grad - mean) * scale).astype(BF16)
        score_grad[s, :cites] = grad.reshape(cites, IT, TOK)
        score_grad[s, cites] = jnp.zeros((IT, TOK), BF16)
        return 0

    lax.fori_loop(0, G, backward, 0, unroll=True)
    sum_start(1)

    for_sibling(0)
    sum_start(0)
    sum_own(1)
    for s in range(G):
        give(s, hgrad_out.at[s], hgrad_ref.at[:, head(b)], out_r.at[0])
        give(s, normed_out.at[s], normed_ref.at[:, head(b)], out_r.at[0])
    sum_step(1, 1)
    sum_own(0)
    sum_step(0, 1)
    for s in range(G):
        grad = score_grad[s, :cites].reshape(cites * IT, TOK)
        dq_out[s] = dot(grad, ksel[s], TN).astype(BF16)
    for s in range(G):
        give(s, dq_out.at[s], qgrad_ref.at[:, head(b)], out_r.at[0])
    for t in range(2, T):
        sum_step(1, t)
        sum_step(0, t)
    sum_end_theirs(1)
    sum_end_theirs(0)
    sum_end(1)
    sum_end(0)

    left_here(k_all.at[pl.ds(0, (Z - 1) * block_rows)], RING)
    left_here(k_all, PAIR)
    left_here(stat_in.at[pl.ds(0, X * Y - 1)], STAT)
    left_here(k_all.at[pl.ds(0, (Z - 1) * block_rows)], SUM_RING)
    left_here(k_all, SUM_PAIR)
    group_rows = 304 * 2

    @pl.when(in_group)
    def _():
        left_here(probs.at[pl.ds(0, G - 1), pl.ds(0, group_rows)], GROUP)

    @pl.when(jnp.logical_not(in_group))
    def _():
        left_here(probs.at[:, pl.ds(0, group_rows)], GROUP)

    landed(probs.at[:, pl.ds(0, 160 * 2)], out_r.at[0])


def leave(*refs):
    sources, places, stages, sems = refs[:5], refs[5:10], refs[10:15], refs[15]
    loads = [
        pltpu.make_async_copy(s, p, sems.at[0, n]) for n, (s, p) in enumerate(zip(sources, stages))
    ]
    stores = [
        pltpu.make_async_copy(s, p, sems.at[1, n]) for n, (s, p) in enumerate(zip(stages, places))
    ]
    for copy in loads:
        copy.start()
    for load, store in zip(loads, stores):
        load.wait()
        store.start()
    for copy in stores:
        copy.wait()


def local(
    Z,
    M,
    hidden_in,
    queries,
    image_kv,
    image_owner,
    citations,
    cite_mask,
    gate_scalars,
    norm_gain,
    upstream,
):
    cites = cite_mask.shape[1]
    n_rows = Z * Y * IMG_DEV
    T = Z // 2
    hbm = pl.BlockSpec(memory_space=pltpu.HBM)
    heads = (G, TOK, HEAD_DIM)
    share = (G * IMG_DEV, IT, HEAD_DIM)
    block = (Y * IMG_DEV, IT, HEAD_DIM)
    quarter = (Y * IMG_DEV // 4, IT, HEAD_DIM)
    keys = cites * IT
    dma = pltpu.SemaphoreType.DMA
    like = lambda v: jax.ShapeDtypeStruct(v.shape, v.dtype)
    results = pl.pallas_call(
        functools.partial(kernel, Z, M, cites),
        out_shape=(like(hidden_in),) * 4 + (like(image_kv),),
        in_specs=[hbm] * 9,
        out_specs=(hbm,) * 5,
        scratch_shapes=[
            pltpu.SMEM((n_rows,), jnp.int32),
            pltpu.SMEM(citations.shape[::-1], jnp.int32),
            pltpu.SMEM((1,), F32),
            pltpu.VMEM((M * G, HEAD_DIM), F32),
            pltpu.VMEM((8, n_rows), jnp.int32),
            pltpu.SMEM((8, n_rows), jnp.int32),
            pltpu.VMEM((n_rows, IT, HEAD_DIM), BF16),
            pltpu.VMEM((n_rows, IT, HEAD_DIM), BF16),
            pltpu.VMEM(heads, BF16),
            pltpu.VMEM(heads, BF16),
            pltpu.VMEM(heads, BF16),
            pltpu.VMEM((G, cites, TOK), jnp.int32),
            pltpu.VMEM((G, keys, HEAD_DIM), BF16),
            pltpu.VMEM((G, keys, HEAD_DIM), BF16),
            pltpu.VMEM((G, keys, TOK), F32),
            pltpu.VMEM((G, cites + 1, IT, TOK), BF16),
            pltpu.VMEM((G, TOK, keys), BF16),
            pltpu.VMEM(heads, BF16),
            pltpu.VMEM(heads, BF16),
            pltpu.VMEM(heads, BF16),
            pltpu.VMEM(heads, BF16),
            pltpu.VMEM(heads, BF16),
            pltpu.VMEM((8, TOK), F32),
            pltpu.VMEM((M // 2 * Y, 8, TOK), F32),
            pltpu.VMEM((G, cites + 1, IT, TOK), BF16),
            pltpu.VMEM((2, T + 1, Y * IMG_DEV * IT, G * TOK), BF16),
            pltpu.VMEM((2, T + 1, Y * IMG_DEV * IT, G * TOK), BF16),
            pltpu.VMEM((2, T) + block, F32),
            pltpu.VMEM((2, T) + block, BF16),
            pltpu.VMEM((2, T) + block, BF16),
            pltpu.VMEM((2, T, 4) + quarter, BF16),
            pltpu.VMEM((2, T, 4) + quarter, BF16),
            pltpu.VMEM((2, 2) + share, BF16),
            pltpu.VMEM((2,) + share, BF16),
            dma((6,)),
            dma((2, 2)),
            dma((2,)),
            dma((2, T, 4)),
            dma((2, 2)),
            dma((1,)),
            dma((1,)),
            dma((2, 2)),
            dma((2, T, 4)),
            dma((2,)),
            dma((5,)),
        ],
        compiler_params=pltpu.CompilerParams(
            collective_id=0, has_side_effects=True, vmem_limit_bytes=VMEM_BYTES
        ),
        name="attend",
    )(
        hidden_in,
        queries,
        image_kv,
        image_owner,
        citations.T,
        cite_mask.T,
        gate_scalars,
        norm_gain.reshape(M * G, HEAD_DIM),
        upstream,
    )
    return pl.pallas_call(
        leave,
        out_shape=tuple(like(v) for v in results),
        in_specs=[hbm] * 5,
        out_specs=(hbm,) * 5,
        scratch_shapes=[pltpu.VMEM(v.shape, v.dtype) for v in results] + [dma((2, 5))],
        compiler_params=pltpu.CompilerParams(vmem_limit_bytes=VMEM_BYTES),
        name="leave",
    )(*results)


def solution(mesh):
    Z = mesh.shape["dp"] // Y
    M = mesh.shape["mp"]
    placed = (
        P("dp", "mp"),
        P("dp", "mp"),
        P("dp", None, None, "mp"),
        P(),
        P(),
        P("dp", None),
        P(),
        P(),
        P("dp", "mp"),
    )
    return jax.shard_map(
        functools.partial(local, Z, M),
        mesh=mesh,
        in_specs=placed,
        out_specs=(
            P("dp", "mp"),
            P("dp", "mp"),
            P("dp", "mp"),
            P("dp", "mp"),
            P("dp", None, None, "mp"),
        ),
        check_vma=False,
    )
```
